32 devices in a mesh: rep: 4 (over z), shard: 8 (over y, x, core).
Axes of the slice: x: 2, y: 2, z: 4, core: 2. Of those that a mesh axis runs over, the one named last changes fastest.
Arguments:
- hidden_acts: bfloat16 [4096, 1024], P(('rep', 'shard')), may hold values from -6 to 6
- out_grads: bfloat16 [4096, 8192], P(('rep', 'shard')), may hold values from -0.1875 to 0.1875
- momentum: float32 [4, 1024, 8192], P('rep', None, 'shard'), may hold values from -6 to 6
- kept: int32 [32], replicated, may hold values from 0 to 4095, as said below
Outputs:
- residual_momentum: float32 [4, 1024, 8192], P('rep', None, 'shard')
- update: bfloat16 [1024, 8192], P(None, 'shard')
The draws below stay inside these ranges and needn't reach their ends.
Inputs may be any that keep to these rules, and one draw needn't show every extreme that they name: `kept`: 32 distinct indices u * 64 + v of a block's coefficients, u the row frequency and v the column frequency; the same list for every block.
All inputs are finite; a program needn't handle non-finite values.
Results may differ from the reference program's by a relative error of at most 0.001.
Values may be sent and summed in bfloat16 or wider, within the bound.
A program may use at most 128 MiB of HBM per device.

```python
import math
import jax
import jax.numpy as jnp
from jax import lax

D = 8192
ROWS = 1024
TOK_DEV = 128
GROUP = 64
KEPT = 32
TOKENS = 4096
REPLICAS = 4
N_REP = 4
N_SHARD = 8


def draw_kept(key, part):
    key = jax.random.fold_in(key, 7)
    first_key, second_key = jax.random.split(key)
    middle = jax.random.permutation(first_key, GROUP * GROUP - 2)[:KEPT - 2].astype(jnp.int32) + 1
    values = jnp.concatenate([jnp.zeros((1,), jnp.int32), middle, jnp.full((1,), GROUP * GROUP - 1, jnp.int32)])
    order = jax.random.permutation(second_key, KEPT)
    return values[order]


def levels(own_key, shape, cuts, low, largest):
    loudness = 1.0
    for dim, shards_of in cuts:
        steps = jax.random.uniform(jax.random.fold_in(jax.random.fold_in(own_key, 6), dim), (shards_of,), jnp.float32, low / len(cuts), largest / len(cuts))
        loudness = loudness * jnp.repeat(jnp.exp(steps), shape[dim] // shards_of).reshape((-1,) + (1,) * (len(shape) - 1 - dim))
    return loudness


def centred(stream_key, dims, spread, bound, cuts=(), held_as=jnp.bfloat16):
    array = spread * jax.random.normal(stream_key, dims, jnp.float32)
    if cuts:
        array = array * levels(stream_key, dims, cuts, -0.22, 0.18)
    return jnp.clip(array, -bound, bound).astype(held_as)


def setup_inputs(seed: int = 0) -> dict:
    seeds = jax.random.split(jax.random.key(seed), 5)
    return {
        "hidden_acts": centred(seeds[0], (TOKENS, ROWS), 1.0, 6.0, ((0, 32),)),
        "out_grads": centred(seeds[1], (TOKENS, D), (TOK_DEV * N_SHARD) ** -0.5, 0.1875, ((0, 32),)),
        "momentum": centred(seeds[2], (REPLICAS, ROWS, D), 1.0, 6.0, ((0, 4), (2, 8)), jnp.float32),
        "kept": draw_kept(jax.random.fold_in(seeds[4], 71), 0),
    }


decay_rate = 0.9

def cosine_matrix(length):
    frequency = jnp.arange(length, dtype=jnp.float32)[:, None]
    position = jnp.arange(length, dtype=jnp.float32)[None, :]
    cosines = jnp.cos(math.pi * (2.0 * position + 1.0) * frequency / (2.0 * length)) * math.sqrt(2.0 / length)
    return cosines * jnp.where(frequency == 0.0, math.sqrt(0.5), 1.0)

def reference(hidden_acts, out_grads, momentum, kept):
    cosines = cosine_matrix(GROUP)
    bands = ROWS // GROUP
    tiles = D // GROUP
    tok_rep = TOK_DEV * N_SHARD

    def to_blocks(field):
        return field.reshape(bands, GROUP, tiles, GROUP).transpose(0, 2, 1, 3)

    def from_blocks(blocks):
        return blocks.transpose(0, 2, 1, 3).reshape(ROWS, D)

    def extract(field):
        spectrum = jnp.einsum('un,abnm,vm->abuv', cosines, to_blocks(field), cosines, precision=lax.Precision.HIGHEST)
        return spectrum.reshape(bands, tiles, GROUP * GROUP)[:, :, kept]

    def restore(values):
        dense = jnp.zeros((bands, tiles, GROUP * GROUP), jnp.float32).at[:, :, kept].set(values)
        spatial = jnp.einsum('un,abuv,vm->abnm', cosines, dense.reshape(bands, tiles, GROUP, GROUP), cosines, precision=lax.Precision.HIGHEST)
        return from_blocks(spatial)

    def per_replica(index):
        acts = lax.dynamic_slice_in_dim(hidden_acts, index * tok_rep, tok_rep, 0)
        grads = lax.dynamic_slice_in_dim(out_grads, index * tok_rep, tok_rep, 0)
        gradient = jnp.dot(acts.T, grads, preferred_element_type=jnp.float32)
        fresh = decay_rate * momentum[index] + gradient
        values = extract(fresh)
        return (fresh - restore(values), values)
    residual, values = lax.map(per_replica, jnp.arange(N_REP, dtype=jnp.int32))
    update = restore(lax.optimization_barrier(jnp.sum(values, axis=0))).astype(jnp.bfloat16)
    return (residual, update)
```

```python
import functools
import math

import jax
import jax.numpy as jnp
import numpy as np
from jax import lax
from jax.experimental import pallas as pl
from jax.experimental.pallas import tpu as pltpu
from jax.sharding import PartitionSpec as P

GROUP = 64
WIDTH = 256
DECAY = 0.9
MESH = pl.DeviceIdType.MESH


def cosine_matrix(length):
    frequency = np.arange(length, dtype=np.float64)[:, None]
    position = np.arange(length, dtype=np.float64)[None, :]
    cosines = np.cos(math.pi * (2.0 * position + 1.0) * frequency / (2.0 * length)) * math.sqrt(2.0 / length)
    return (cosines * np.where(frequency == 0.0, math.sqrt(0.5), 1.0)).astype(np.float32)


def flip(index, bits):
    out = index
    power = 1
    while power <= bits:
        if bits & power:
            out = out + power - 2 * power * ((index // power) % 2)
        power *= 2
    return out


def split(x):
    high = x.astype(jnp.bfloat16)
    return high, (x - high.astype(jnp.float32)).astype(jnp.bfloat16)


def dot_nt(a, b):
    return lax.dot_general(a, b, (((1,), (1,)), ((), ())), preferred_element_type=jnp.float32)


def dot_nn(a, b):
    return lax.dot_general(a, b, (((1,), (0,)), ((), ())), preferred_element_type=jnp.float32)


def exchange_kernel(
    shards, reps, chunks, kept_count,
    kept_ref, cos_t_ref, cos_tiled_ref, acts_ref, grads_ref, momentum_ref,
    fresh_ref, coeffs_ref, total_ref, right_ref, left_ref,
    own_acts, acts_t, grads_all, fresh, gathered,
    acts_send, acts_recv, grads_send, grads_recv, rep_send, rep_recv,
    local_acts, local_grads, local_mom, out_sem,
):
    rep = lax.axis_index("rep")
    me = lax.axis_index("shard")
    sibling = flip(me, 1)
    tok, rows = acts_ref.shape
    columns = chunks * WIDTH
    tiles = WIDTH // GROUP
    lanes = tiles * kept_count

    pltpu.make_async_copy(acts_ref, own_acts, local_acts).start()

    def own_grads(j):
        return pltpu.make_async_copy(
            grads_ref.at[:, pl.ds(pl.multiple_of(me * columns + j * WIDTH, WIDTH), WIDTH)],
            grads_all.at[j, pl.ds(0, tok), :],
            local_grads.at[j],
        )

    def load_momentum(j):
        return pltpu.make_async_copy(
            momentum_ref.at[0, :, pl.ds(pl.multiple_of(j * WIDTH, WIDTH), WIDTH)], fresh.at[j], local_mom.at[j]
        )

    def store_fresh(j):
        return pltpu.make_async_copy(
            fresh.at[j], fresh_ref.at[:, pl.ds(pl.multiple_of(j * WIDTH, WIDTH), WIDTH)], out_sem.at[j]
        )

    barrier = pltpu.get_barrier_semaphore()
    for o in range(1, shards):
        pl.semaphore_signal(barrier, inc=1, device_id=(rep, flip(me, o)), device_id_type=MESH)
    for q in range(1, reps):
        pl.semaphore_signal(barrier, inc=1, device_id=(flip(rep, q), me), device_id_type=MESH)

    def send_grads(o, j):
        peer = flip(me, o)
        return pltpu.make_async_remote_copy(
            src_ref=grads_ref.at[:, pl.ds(pl.multiple_of(peer * columns + j * WIDTH, WIDTH), WIDTH)],
            dst_ref=grads_all.at[j, pl.ds(o * tok, tok), :],
            send_sem=grads_send.at[j, o],
            recv_sem=grads_recv.at[j, o],
            device_id=(rep, peer),
            device_id_type=MESH,
        )

    def acts_slot(o):
        return acts_t.at[:, pl.ds(o * tok, tok)]

    def send_acts(o):
        source = acts_slot(0 if o % 2 == 0 else o - 1)
        peer = flip(me, o) if o % 2 == 0 else sibling
        return pltpu.make_async_remote_copy(
            src_ref=source,
            dst_ref=acts_slot(o),
            send_sem=acts_send.at[o],
            recv_sem=acts_recv.at[o],
            device_id=(rep, peer),
            device_id_type=MESH,
        )

    def send_coeffs(q, j):
        return pltpu.make_async_remote_copy(
            src_ref=coeffs_ref.at[j],
            dst_ref=gathered.at[j, q],
            send_sem=rep_send.at[j, q],
            recv_sem=rep_recv.at[j, q],
            device_id=(flip(rep, q), me),
            device_id_type=MESH,
        )

    pltpu.make_async_copy(acts_ref, own_acts, local_acts).wait()
    acts_t[:, pl.ds(0, tok)] = own_acts[...].T
    pl.semaphore_wait(barrier, shards - 1 + reps - 1)

    for o in range(shards - 2, 1, -2):
        send_acts(o).start()
    send_acts(1).start()
    for j in range(chunks):
        for o in range(shards - 1, 0, -1):
            send_grads(o, j).start()
    for j in range(chunks):
        own_grads(j).start()
        load_momentum(j).start()

    row = lax.broadcasted_iota(jnp.int32, (lanes, GROUP), 0) % kept_count
    freq_v = lax.broadcasted_iota(jnp.int32, (lanes, GROUP), 1)
    lane = lax.broadcasted_iota(jnp.int32, (GROUP, lanes), 1) % kept_count
    freq_u = lax.broadcasted_iota(jnp.int32, (GROUP, lanes), 0)
    hot_v = jnp.zeros((lanes, GROUP), jnp.float32)
    hot_u = jnp.zeros((GROUP, lanes), jnp.float32)
    for k in range(kept_count):
        index = kept_ref[k]
        hot_v = jnp.where((row == k) & (freq_v == index % GROUP), 1.0, hot_v)
        hot_u = jnp.where((lane == k) & (freq_u == index // GROUP), 1.0, hot_u)
    right = jnp.dot(
        hot_v, cos_tiled_ref[...], precision=lax.Precision.HIGHEST, preferred_element_type=jnp.float32
    )
    same_tile = (
        lax.broadcasted_iota(jnp.int32, (lanes, WIDTH), 0) // kept_count
        == lax.broadcasted_iota(jnp.int32, (lanes, WIDTH), 1) // GROUP
    )
    right_ref[...] = jnp.where(same_tile, right, 0.0)
    left_ref[...] = jnp.dot(
        cos_t_ref[...], hot_u, precision=lax.Precision.HIGHEST, preferred_element_type=jnp.float32
    )

    for o in range(2, shards, 2):
        send_acts(o).wait_recv()
        send_acts(o + 1).start()
    for o in range(1, shards, 2):
        send_acts(o).wait_recv()

    half = rows // 2
    bands = half // GROUP

    def chunk(j, carry):
        for o in range(1, shards):
            send_grads(o, j).wait_recv()
        own_grads(j).wait()
        load_momentum(j).wait()
        right_high, right_low = split(right_ref[...])
        right_both = jnp.concatenate([right_high, right_low], axis=0)
        left = left_ref[...]
        for t in range(2):
            part = pl.ds(t * half, half)
            gradient = dot_nn(acts_t[part, :], grads_all[j])
            value = DECAY * fresh[j, part, :] + gradient
            fresh[j, part, :] = value
            high, low = split(value)
            both = dot_nt(high, right_both)
            done = both[:, :lanes] + both[:, lanes:] + dot_nt(low, right_high)
            coeffs_ref[j, pl.ds(t * bands, bands), :] = jnp.sum(
                done.reshape(bands, GROUP, lanes) * left[None], axis=1
            )
        for q in range(1, reps):
            send_coeffs(q, j).start()
        store_fresh(j).start()
        return carry

    lax.fori_loop(0, chunks, chunk, 0)

    def finish(j, carry):
        for q in range(1, reps):
            send_coeffs(q, j).wait_recv()
        terms = [coeffs_ref[j]] + [gathered[j, q] for q in range(1, reps)]
        while len(terms) > 1:
            terms = [terms[i] + terms[i + 1] for i in range(0, len(terms), 2)]
        total_ref[j] = terms[0]
        for q in range(1, reps):
            send_coeffs(q, j).wait_send()
        for o in range(1, shards):
            send_grads(o, j).wait_send()
        store_fresh(j).wait()
        return carry

    lax.fori_loop(0, chunks, finish, 0)
    for o in range(1, shards):
        send_acts(o).wait_send()


def decode_kernel(fresh_ref, coeffs_ref, total_ref, right_ref, left_ref, residual_ref, update_ref):
    right_high, right_low = split(right_ref[...])
    twice = jnp.concatenate([right_high, right_high], axis=0)
    left = left_ref[...]
    rows = fresh_ref.shape[0]
    lanes = left.shape[1]
    bands = rows // GROUP

    def decode(values):
        dense = (values[:, None, :] * left[None]).reshape(rows, lanes)
        high, low = split(dense)
        return dot_nn(jnp.concatenate([high, low], axis=1), twice) + dot_nn(high, right_low)

    residual_ref[0] = fresh_ref[...] - decode(coeffs_ref[0])
    update_ref[...] = decode(total_ref[0]).astype(jnp.bfloat16)


def on_device(shards, reps, hidden_acts, out_grads, momentum, kept):
    tok, rows = hidden_acts.shape
    columns = momentum.shape[2]
    chunks = columns // WIDTH
    kept_count = kept.shape[0]
    tiles = WIDTH // GROUP
    lanes = tiles * kept_count
    bands = rows // GROUP
    cosines = cosine_matrix(GROUP)
    f32 = jnp.float32
    any_space = pl.BlockSpec(memory_space=pl.ANY)
    vmem = pl.BlockSpec(memory_space=pltpu.VMEM)
    fresh, coeffs, total, right, left = pl.pallas_call(
        functools.partial(exchange_kernel, shards, reps, chunks, kept_count),
        out_shape=(
            jax.ShapeDtypeStruct((rows, columns), f32),
            jax.ShapeDtypeStruct((chunks, bands, lanes), f32),
            jax.ShapeDtypeStruct((chunks, bands, lanes), f32),
            jax.ShapeDtypeStruct((lanes, WIDTH), f32),
            jax.ShapeDtypeStruct((GROUP, lanes), f32),
        ),
        in_specs=[pl.BlockSpec(memory_space=pltpu.SMEM), vmem, vmem, any_space, any_space, any_space],
        out_specs=(any_space, vmem, vmem, vmem, vmem),
        scratch_shapes=[
            pltpu.VMEM((tok, rows), jnp.bfloat16),
            pltpu.VMEM((rows, shards * tok), jnp.bfloat16),
            pltpu.VMEM((chunks, shards * tok, WIDTH), jnp.bfloat16),
            pltpu.VMEM((chunks, rows, WIDTH), f32),
            pltpu.VMEM((chunks, reps, bands, lanes), f32),
            pltpu.SemaphoreType.DMA((shards,)),
            pltpu.SemaphoreType.DMA((shards,)),
            pltpu.SemaphoreType.DMA((chunks, shards)),
            pltpu.SemaphoreType.DMA((chunks, shards)),
            pltpu.SemaphoreType.DMA((chunks, reps)),
            pltpu.SemaphoreType.DMA((chunks, reps)),
            pltpu.SemaphoreType.DMA,
            pltpu.SemaphoreType.DMA((chunks,)),
            pltpu.SemaphoreType.DMA((chunks,)),
            pltpu.SemaphoreType.DMA((chunks,)),
        ],
        compiler_params=pltpu.CompilerParams(
            collective_id=0, has_side_effects=True, vmem_limit_bytes=48 * 2**20
        ),
        name="exchange",
    )(
        kept,
        jnp.asarray(np.ascontiguousarray(cosines.T)),
        jnp.asarray(np.tile(cosines, (1, tiles))),
        hidden_acts,
        out_grads,
        momentum,
    )
    residual, update = pl.pallas_call(
        decode_kernel,
        grid=(2, chunks),
        out_shape=(
            jax.ShapeDtypeStruct((1, rows, columns), f32),
            jax.ShapeDtypeStruct((rows, columns), jnp.bfloat16),
        ),
        in_specs=[
            pl.BlockSpec((rows // 2, WIDTH), lambda i, j: (i, j)),
            pl.BlockSpec((1, bands // 2, lanes), lambda i, j: (j, i, 0)),
            pl.BlockSpec((1, bands // 2, lanes), lambda i, j: (j, i, 0)),
            pl.BlockSpec((lanes, WIDTH), lambda i, j: (0, 0)),
            pl.BlockSpec((GROUP, lanes), lambda i, j: (0, 0)),
        ],
        out_specs=(
            pl.BlockSpec((1, rows // 2, WIDTH), lambda i, j: (0, i, j)),
            pl.BlockSpec((rows // 2, WIDTH), lambda i, j: (i, j)),
        ),
        compiler_params=pltpu.CompilerParams(vmem_limit_bytes=32 * 2**20),
        name="decode",
    )(fresh, coeffs, total, right, left)
    return residual, update


def solution(mesh):
    placed = (P(("rep", "shard"), None), P(("rep", "shard"), None), P("rep", None, "shard"), P())
    return jax.shard_map(
        functools.partial(on_device, mesh.shape["shard"], mesh.shape["rep"]),
        mesh=mesh,
        in_specs=placed,
        out_specs=(P("rep", None, "shard"), P(None, "shard")),
        check_vma=False,
    )
```

```python
import functools
import math

import jax
import jax.numpy as jnp
import numpy as np
from jax import lax
from jax.experimental import pallas as pl
from jax.experimental.pallas import tpu as pltpu
from jax.sharding import PartitionSpec as P

GROUP = 64
WIDTH = 256
DECAY = 0.9
MESH = pl.DeviceIdType.MESH


def cosine_matrix(length):
    frequency = np.arange(length, dtype=np.float64)[:, None]
    position = np.arange(length, dtype=np.float64)[None, :]
    cosines = np.cos(math.pi * (2.0 * position + 1.0) * frequency / (2.0 * length)) * math.sqrt(2.0 / length)
    return (cosines * np.where(frequency == 0.0, math.sqrt(0.5), 1.0)).astype(np.float32)


def flip(index, bits):
    out = index
    power = 1
    while power <= bits:
        if bits & power:
            out = out + power - 2 * power * ((index // power) % 2)
        power *= 2
    return out


def split(x):
    high = x.astype(jnp.bfloat16)
    return high, (x - high.astype(jnp.float32)).astype(jnp.bfloat16)


def dot_nt(a, b):
    return lax.dot_general(a, b, (((1,), (1,)), ((), ())), preferred_element_type=jnp.float32)


def dot_nn(a, b):
    return lax.dot_general(a, b, (((1,), (0,)), ((), ())), preferred_element_type=jnp.float32)


def decode(values, left, right_high, right_low):
    bands, lanes = values.shape
    dense = (values[:, None, :] * left[None]).reshape(bands * GROUP, lanes)
    high, low = split(dense)
    twice = jnp.concatenate([right_high, right_high], axis=0)
    return dot_nn(jnp.concatenate([high, low], axis=1), twice) + dot_nn(high, right_low)


def exchange_kernel(
    shards, reps, chunks, kept_count,
    kept_hbm, table_hbm, acts_ref, grads_ref, momentum_ref,
    residual_ref, update_ref, total_ref, right_ref, left_ref,
    kept_ref, table, own_acts, acts_t, grads_all, coeffs, gathered,
    acts_send, acts_recv, grads_send, grads_recv, rep_send, rep_recv,
    local_kept, local_table, local_acts, local_grads, local_mom,
):
    rep = lax.axis_index("rep")
    me = lax.axis_index("shard")
    core = me % 2
    tok, rows = acts_ref.shape
    columns = chunks * WIDTH
    tiles = WIDTH // GROUP
    lanes = tiles * kept_count
    chips = shards // 2
    square = chips == 4
    offsets = sorted(range(1, chips), key=lambda c: c == 2)

    load_acts = pltpu.make_async_copy(acts_ref, own_acts, local_acts)
    load_kept = pltpu.make_async_copy(kept_hbm, kept_ref, local_kept)
    load_table = pltpu.make_async_copy(table_hbm, table, local_table)
    load_acts.start()

    barrier = pltpu.get_barrier_semaphore()
    for o in range(1, shards):
        pl.semaphore_signal(barrier, inc=1, device_id=(rep, flip(me, o)), device_id_type=MESH)
    for q in range(1, reps):
        pl.semaphore_signal(barrier, inc=1, device_id=(flip(rep, q), me), device_id_type=MESH)
    load_kept.start()
    load_table.start()

    def own_grads(j):
        return pltpu.make_async_copy(
            grads_ref.at[:, pl.ds(pl.multiple_of(me * columns + j * WIDTH, WIDTH), WIDTH)],
            grads_all.at[j, pl.ds(0, tok), :],
            local_grads.at[j],
        )

    def load_momentum(j):
        return pltpu.make_async_copy(
            momentum_ref.at[0, :, pl.ds(pl.multiple_of(j * WIDTH, WIDTH), WIDTH)],
            residual_ref.at[j],
            local_mom.at[j],
        )

    def send_grads(o, j):
        peer = flip(me, o)
        return pltpu.make_async_remote_copy(
            src_ref=grads_ref.at[:, pl.ds(pl.multiple_of(peer * columns + j * WIDTH, WIDTH), WIDTH)],
            dst_ref=grads_all.at[j, pl.ds(o * tok, tok), :],
            send_sem=grads_send.at[j, o],
            recv_sem=grads_recv.at[j, o],
            device_id=(rep, peer),
            device_id_type=MESH,
        )

    def start_grads(j):
        for own, order in ((0, offsets), (1, offsets[::-1])):
            @pl.when(core == own)
            def _():
                for c in order:
                    send_grads(2 * c, j).start()
                    send_grads(2 * c + 1, j).start()
                send_grads(1, j).start()

    def acts_copy(source, slot, bits, low, count, sem):
        return pltpu.make_async_remote_copy(
            src_ref=acts_t.at[pl.ds(low, count), pl.ds(source * tok, tok)],
            dst_ref=acts_t.at[pl.ds(low, count), pl.ds(slot * tok, tok)],
            send_sem=acts_send.at[sem],
            recv_sem=acts_recv.at[sem],
            device_id=(rep, flip(me, bits)),
            device_id_type=MESH,
        )

    def send_direct(o):
        return acts_copy(0, o, o, 0, rows, o)

    def send_sibling(o):
        return acts_copy(o, o + 1, 1, 0, rows, o + 1)

    def send_across(bits):
        if bits == 2:
            return acts_copy(4, 6, 2, rows // 2, rows // 2, shards)
        return acts_copy(2, 6, 4, 0, rows // 2, 6)

    def send_coeffs(q, j):
        return pltpu.make_async_remote_copy(
            src_ref=coeffs.at[j],
            dst_ref=gathered.at[j, q],
            send_sem=rep_send.at[j, q],
            recv_sem=rep_recv.at[j, q],
            device_id=(flip(rep, q), me),
            device_id_type=MESH,
        )

    load_acts.wait()
    acts_t[:, pl.ds(0, tok)] = own_acts[...].T
    pl.semaphore_wait(barrier, shards - 1 + reps - 1)

    direct = [c for c in offsets if not (square and c == 3)]
    for own, order in ((0, direct), (1, direct[::-1])):
        @pl.when(core == own)
        def _():
            for c in order:
                send_direct(2 * c).start()
    send_sibling(0).start()
    start_grads(0)
    for j in range(chunks):
        own_grads(j).start()
        load_momentum(j).start()

    load_kept.wait()
    load_table.wait()
    row = lax.broadcasted_iota(jnp.int32, (lanes, GROUP), 0) % kept_count
    freq_v = lax.broadcasted_iota(jnp.int32, (lanes, GROUP), 1)
    lane = lax.broadcasted_iota(jnp.int32, (GROUP, lanes), 1) % kept_count
    freq_u = lax.broadcasted_iota(jnp.int32, (GROUP, lanes), 0)
    hot_v = jnp.zeros((lanes, GROUP), jnp.float32)
    hot_u = jnp.zeros((GROUP, lanes), jnp.float32)
    for k in range(kept_count):
        index = kept_ref[k]
        hot_v = jnp.where((row == k) & (freq_v == index % GROUP), 1.0, hot_v)
        hot_u = jnp.where((lane == k) & (freq_u == index // GROUP), 1.0, hot_u)
    right = jnp.dot(
        hot_v, table[:, :WIDTH], precision=lax.Precision.HIGHEST, preferred_element_type=jnp.float32
    )
    same_tile = (
        lax.broadcasted_iota(jnp.int32, (lanes, WIDTH), 0) // kept_count
        == lax.broadcasted_iota(jnp.int32, (lanes, WIDTH), 1) // GROUP
    )
    right_ref[...] = jnp.where(same_tile, right, 0.0)
    left_ref[...] = jnp.dot(
        table[:, WIDTH:WIDTH + GROUP], hot_u, precision=lax.Precision.HIGHEST, preferred_element_type=jnp.float32
    )

    for own, order in ((0, direct), (1, direct[::-1])):
        @pl.when(core == own)
        def _():
            for c in order:
                send_direct(2 * c).wait_recv()
                if square:
                    send_across(6 - 2 * c).start()
                send_sibling(2 * c).start()
    ahead = min(3, chunks)
    for j in range(1, min(2, chunks)):
        start_grads(j)
    if square:
        send_across(4).wait_recv()
        send_across(2).wait_recv()
        send_sibling(6).start()
    for j in range(2, ahead):
        start_grads(j)
    for o in range(0, shards, 2):
        send_sibling(o).wait_recv()

    half = rows // 2
    bands = half // GROUP

    def finish(j, with_update):
        for q in range(1, reps):
            send_coeffs(q, j).wait_recv()
        terms = [coeffs[j]] + [gathered[j, q] for q in range(1, reps)]
        while len(terms) > 1:
            terms = [terms[i] + terms[i + 1] for i in range(0, len(terms), 2)]
        total_ref[...] = terms[0]
        if with_update:
            right_high, right_low = split(right_ref[...])
            for t in range(2):
                values = total_ref[pl.ds(t * bands, bands), :]
                update_ref[j, pl.ds(t * half, half), :] = decode(
                    values, left_ref[...], right_high, right_low
                ).astype(jnp.bfloat16)

    def chunk(j, carry):
        for o in range(1, shards):
            send_grads(o, j).wait_recv()

        @pl.when(j + ahead < chunks)
        def _():
            start_grads(j + ahead)

        own_grads(j).wait()
        load_momentum(j).wait()
        right_high, right_low = split(right_ref[...])
        right_both = jnp.concatenate([right_high, right_low], axis=0)
        left = left_ref[...]
        for t in range(2):
            part = pl.ds(t * half, half)
            gradient = dot_nn(acts_t[part, :], grads_all[j])
            value = DECAY * residual_ref[j, part, :] + gradient
            residual_ref[j, part, :] = value
            high, low = split(value)
            both = dot_nt(high, right_both)
            done = both[:, :lanes] + both[:, lanes:] + dot_nt(low, right_high)
            coeffs[j, pl.ds(t * bands, bands), :] = jnp.sum(
                done.reshape(bands, GROUP, lanes) * left[None], axis=1
            )
        for q in range(1, reps):
            send_coeffs(q, j).start()
        for t in range(2):
            part = pl.ds(t * half, half)
            values = coeffs[j, pl.ds(t * bands, bands), :]
            residual_ref[j, part, :] = residual_ref[j, part, :] - decode(values, left, right_high, right_low)

        @pl.when(j > 0)
        def _():
            finish(j - 1, True)

        return carry

    lax.fori_loop(0, chunks, chunk, 0)

    def drain(j, carry):
        for o in range(1, shards):
            send_grads(o, j).wait_send()
        return carry

    lax.fori_loop(0, chunks, drain, 0)
    for c in direct:
        send_direct(2 * c).wait_send()
    for o in range(0, shards, 2):
        send_sibling(o).wait_send()
    if square:
        send_across(2).wait_send()
        send_across(4).wait_send()
    finish(chunks - 1, False)
    for j in range(chunks):
        for q in range(1, reps):
            send_coeffs(q, j).wait_send()


def store_kernel(
    residual_ref, update_ref, total_ref, right_ref, left_ref, residual_out, update_out, last, residual_sem, update_sem
):
    chunks, rows, _ = residual_ref.shape

    def store(source, target, sem, j):
        return pltpu.make_async_copy(source, target.at[:, pl.ds(j * WIDTH, WIDTH)], sem.at[j])

    copies = [store(update_ref.at[j], update_out, update_sem, j) for j in range(chunks - 1)]
    copies += [store(residual_ref.at[j], residual_out.at[0], residual_sem, j) for j in range(chunks)]
    for copy in copies:
        copy.start()
    right_high, right_low = split(right_ref[...])
    last[...] = decode(total_ref[...], left_ref[...], right_high, right_low).astype(jnp.bfloat16)
    copies.append(store(last, update_out, update_sem, chunks - 1))
    copies[-1].start()
    for copy in copies:
        copy.wait()


def on_device(shards, reps, hidden_acts, out_grads, momentum, kept):
    tok, rows = hidden_acts.shape
    columns = momentum.shape[2]
    chunks = columns // WIDTH
    kept_count = kept.shape[0]
    tiles = WIDTH // GROUP
    lanes = tiles * kept_count
    bands = rows // GROUP
    cosines = cosine_matrix(GROUP)
    table = np.concatenate(
        [np.tile(cosines, (1, tiles)), cosines.T, np.zeros((GROUP, 128 - GROUP), np.float32)], axis=1
    )
    f32 = jnp.float32
    hbm = pl.BlockSpec(memory_space=pltpu.HBM)
    vmem = pl.BlockSpec(memory_space=pltpu.VMEM)
    in_hbm = functools.partial(pltpu.with_memory_space_constraint, memory_space=pltpu.HBM)
    kept_parts = pl.pallas_call(
        functools.partial(exchange_kernel, shards, reps, chunks, kept_count),
        out_shape=(
            jax.ShapeDtypeStruct((chunks, rows, WIDTH), f32),
            jax.ShapeDtypeStruct((chunks, rows, WIDTH), jnp.bfloat16),
            jax.ShapeDtypeStruct((bands, lanes), f32),
            jax.ShapeDtypeStruct((lanes, WIDTH), f32),
            jax.ShapeDtypeStruct((GROUP, lanes), f32),
        ),
        in_specs=[hbm] * 5,
        out_specs=(vmem,) * 5,
        scratch_shapes=[
            pltpu.SMEM((kept_count,), jnp.int32),
            pltpu.VMEM(table.shape, f32),
            pltpu.VMEM((tok, rows), jnp.bfloat16),
            pltpu.VMEM((rows, shards * tok), jnp.bfloat16),
            pltpu.VMEM((chunks, shards * tok, WIDTH), jnp.bfloat16),
            pltpu.VMEM((chunks, bands, lanes), f32),
            pltpu.VMEM((chunks, reps, bands, lanes), f32),
            pltpu.SemaphoreType.DMA((shards + 1,)),
            pltpu.SemaphoreType.DMA((shards + 1,)),
            pltpu.SemaphoreType.DMA((chunks, shards)),
            pltpu.SemaphoreType.DMA((chunks, shards)),
            pltpu.SemaphoreType.DMA((chunks, reps)),
            pltpu.SemaphoreType.DMA((chunks, reps)),
            pltpu.SemaphoreType.DMA,
            pltpu.SemaphoreType.DMA,
            pltpu.SemaphoreType.DMA,
            pltpu.SemaphoreType.DMA((chunks,)),
            pltpu.SemaphoreType.DMA((chunks,)),
        ],
        compiler_params=pltpu.CompilerParams(
            collective_id=0, has_side_effects=True, vmem_limit_bytes=40 * 2**20
        ),
        name="exchange",
    )(*(in_hbm(x) for x in (kept, jnp.asarray(table), hidden_acts, out_grads, momentum)))
    return pl.pallas_call(
        store_kernel,
        out_shape=(
            jax.ShapeDtypeStruct((1, rows, columns), f32),
            jax.ShapeDtypeStruct((rows, columns), jnp.bfloat16),
        ),
        in_specs=[vmem] * 5,
        out_specs=(hbm, hbm),
        scratch_shapes=[
            pltpu.VMEM((rows, WIDTH), jnp.bfloat16),
            pltpu.SemaphoreType.DMA((chunks,)),
            pltpu.SemaphoreType.DMA((chunks,)),
        ],
        compiler_params=pltpu.CompilerParams(vmem_limit_bytes=24 * 2**20),
        name="store",
    )(*kept_parts)


def solution(mesh):
    placed = (P(("rep", "shard"), None), P(("rep", "shard"), None), P("rep", None, "shard"), P())
    return jax.shard_map(
        functools.partial(on_device, mesh.shape["shard"], mesh.shape["rep"]),
        mesh=mesh,
        in_specs=placed,
        out_specs=(P("rep", None, "shard"), P(None, "shard")),
        check_vma=False,
    )
```

```python
import functools
import math

import jax
import jax.numpy as jnp
import numpy as np
from jax import lax
from jax.experimental import pallas as pl
from jax.experimental.pallas import tpu as pltpu
from jax.sharding import PartitionSpec as P

GROUP = 64
WIDTH = 256
DECAY = 0.9
MESH = pl.DeviceIdType.MESH


def cosine_matrix(length):
    frequency = np.arange(length, dtype=np.float64)[:, None]
    position = np.arange(length, dtype=np.float64)[None, :]
    cosines = np.cos(math.pi * (2.0 * position + 1.0) * frequency / (2.0 * length)) * math.sqrt(2.0 / length)
    return (cosines * np.where(frequency == 0.0, math.sqrt(0.5), 1.0)).astype(np.float32)


def flip(index, bits):
    out = index
    power = 1
    while power <= bits:
        if bits & power:
            out = out + power - 2 * power * ((index // power) % 2)
        power *= 2
    return out


def split(x):
    high = x.astype(jnp.bfloat16)
    return high, (x - high.astype(jnp.float32)).astype(jnp.bfloat16)


def dot_nt(a, b):
    return lax.dot_general(a, b, (((1,), (1,)), ((), ())), preferred_element_type=jnp.float32)


def dot_nn(a, b):
    return lax.dot_general(a, b, (((1,), (0,)), ((), ())), preferred_element_type=jnp.float32)


def decode(values, left, right_high, right_low):
    bands, lanes = values.shape
    dense = (values[:, None, :] * left[None]).reshape(bands * GROUP, lanes)
    high, low = split(dense)
    twice = jnp.concatenate([right_high, right_high], axis=0)
    return dot_nn(jnp.concatenate([high, low], axis=1), twice) + dot_nn(high, right_low)


def exchange_kernel(
    shards, reps, chunks, kept_count,
    kept_hbm, table_hbm, acts_ref, grads_ref, momentum_ref,
    residual_ref, update_ref, total_ref, right_ref, left_ref,
    kept_ref, table, own_acts, acts_t, grads_all, coeffs, gathered,
    acts_send, acts_recv, grads_send, grads_recv, rep_send, rep_recv,
    local_kept, local_table, local_acts, local_grads, local_mom,
):
    rep = lax.axis_index("rep")
    me = lax.axis_index("shard")
    core = me % 2
    tok, rows = acts_ref.shape
    columns = chunks * WIDTH
    tiles = WIDTH // GROUP
    lanes = tiles * kept_count
    chips = shards // 2
    square = chips == 4
    offsets = sorted(range(1, chips), key=lambda c: c == 2)

    load_acts = pltpu.make_async_copy(acts_ref, own_acts, local_acts)
    load_kept = pltpu.make_async_copy(kept_hbm, kept_ref, local_kept)
    load_table = pltpu.make_async_copy(table_hbm, table, local_table)
    load_acts.start()

    barrier = pltpu.get_barrier_semaphore()
    for o in range(1, shards):
        pl.semaphore_signal(barrier, inc=1, device_id=(rep, flip(me, o)), device_id_type=MESH)
    for q in range(1, reps):
        pl.semaphore_signal(barrier, inc=1, device_id=(flip(rep, q), me), device_id_type=MESH)
    load_kept.start()
    load_table.start()

    def own_grads(j):
        return pltpu.make_async_copy(
            grads_ref.at[:, pl.ds(pl.multiple_of(me * columns + j * WIDTH, WIDTH), WIDTH)],
            grads_all.at[j, pl.ds(0, tok), :],
            local_grads.at[j],
        )

    def load_momentum(j):
        return pltpu.make_async_copy(
            momentum_ref.at[0, :, pl.ds(pl.multiple_of(j * WIDTH, WIDTH), WIDTH)],
            residual_ref.at[j],
            local_mom.at[j],
        )

    def send_grads(o, j):
        peer = flip(me, o)
        return pltpu.make_async_remote_copy(
            src_ref=grads_ref.at[:, pl.ds(pl.multiple_of(peer * columns + j * WIDTH, WIDTH), WIDTH)],
            dst_ref=grads_all.at[j, pl.ds(o * tok, tok), :],
            send_sem=grads_send.at[j, o],
            recv_sem=grads_recv.at[j, o],
            device_id=(rep, peer),
            device_id_type=MESH,
        )

    def start_grads(j, some):
        for own, order in ((0, some), (1, some[::-1])):
            @pl.when(core == own)
            def _():
                for c in order:
                    send_grads(2 * c, j).start()
                    send_grads(2 * c + 1, j).start()
        if 1 in some:
            send_grads(1, j).start()

    def acts_copy(source, slot, bits, low, count, sem):
        return pltpu.make_async_remote_copy(
            src_ref=acts_t.at[pl.ds(low, count), pl.ds(source * tok, tok)],
            dst_ref=acts_t.at[pl.ds(low, count), pl.ds(slot * tok, tok)],
            send_sem=acts_send.at[sem],
            recv_sem=acts_recv.at[sem],
            device_id=(rep, flip(me, bits)),
            device_id_type=MESH,
        )

    def send_direct(o):
        return acts_copy(0, o, o, 0, rows, o)

    def send_sibling(o):
        return acts_copy(o, o + 1, 1, 0, rows, o + 1)

    def send_across(bits):
        if bits == 2:
            return acts_copy(4, 6, 2, rows // 2, rows // 2, shards)
        return acts_copy(2, 6, 4, 0, rows // 2, 6)

    def send_coeffs(q, j):
        return pltpu.make_async_remote_copy(
            src_ref=coeffs.at[j],
            dst_ref=gathered.at[j, q],
            send_sem=rep_send.at[j, q],
            recv_sem=rep_recv.at[j, q],
            device_id=(flip(rep, q), me),
            device_id_type=MESH,
        )

    direct = [c for c in offsets if not (square and c == 3)]
    across = [c for c in offsets if c not in direct]
    pl.semaphore_wait(barrier, shards - 1 + reps - 1)
    start_grads(0, across)
    load_acts.wait()
    acts_t[:, pl.ds(0, tok)] = own_acts[...].T
    for own, order in ((0, direct), (1, direct[::-1])):
        @pl.when(core == own)
        def _():
            for c in order:
                send_direct(2 * c).start()
    send_sibling(0).start()
    start_grads(0, direct)
    for j in range(1, min(2, chunks)):
        start_grads(j, offsets)
    for j in range(chunks):
        own_grads(j).start()
        load_momentum(j).start()

    load_kept.wait()
    load_table.wait()
    row = lax.broadcasted_iota(jnp.int32, (lanes, GROUP), 0) % kept_count
    freq_v = lax.broadcasted_iota(jnp.int32, (lanes, GROUP), 1)
    lane = lax.broadcasted_iota(jnp.int32, (GROUP, lanes), 1) % kept_count
    freq_u = lax.broadcasted_iota(jnp.int32, (GROUP, lanes), 0)
    hot_v = jnp.zeros((lanes, GROUP), jnp.float32)
    hot_u = jnp.zeros((GROUP, lanes), jnp.float32)
    for k in range(kept_count):
        index = kept_ref[k]
        hot_v = jnp.where((row == k) & (freq_v == index % GROUP), 1.0, hot_v)
        hot_u = jnp.where((lane == k) & (freq_u == index // GROUP), 1.0, hot_u)
    right = jnp.dot(
        hot_v, table[:, :WIDTH], precision=lax.Precision.HIGHEST, preferred_element_type=jnp.float32
    )
    same_tile = (
        lax.broadcasted_iota(jnp.int32, (lanes, WIDTH), 0) // kept_count
        == lax.broadcasted_iota(jnp.int32, (lanes, WIDTH), 1) // GROUP
    )
    right_ref[...] = jnp.where(same_tile, right, 0.0)
    left_ref[...] = jnp.dot(
        table[:, WIDTH:WIDTH + GROUP], hot_u, precision=lax.Precision.HIGHEST, preferred_element_type=jnp.float32
    )

    for own, order in ((0, direct), (1, direct[::-1])):
        @pl.when(core == own)
        def _():
            for c in order:
                send_direct(2 * c).wait_recv()
                if square:
                    send_across(6 - 2 * c).start()
                send_sibling(2 * c).start()
    ahead = min(4, chunks)
    for j in range(2, min(3, chunks)):
        start_grads(j, offsets)
    if square:
        send_across(4).wait_recv()
        send_across(2).wait_recv()
        send_sibling(6).start()
    for j in range(3, ahead):
        start_grads(j, offsets)
    for o in range(0, shards, 2):
        send_sibling(o).wait_recv()

    half = rows // 2
    bands = half // GROUP

    def finish(j, with_update):
        for q in range(1, reps):
            send_coeffs(q, j).wait_recv()
        terms = [coeffs[j]] + [gathered[j, q] for q in range(1, reps)]
        while len(terms) > 1:
            terms = [terms[i] + terms[i + 1] for i in range(0, len(terms), 2)]
        total_ref[...] = terms[0]
        if with_update:
            right_high, right_low = split(right_ref[...])
            for t in range(2):
                values = total_ref[pl.ds(t * bands, bands), :]
                update_ref[j, pl.ds(t * half, half), :] = decode(
                    values, left_ref[...], right_high, right_low
                ).astype(jnp.bfloat16)

    def chunk(j, carry):
        for o in range(1, shards):
            send_grads(o, j).wait_recv()

        @pl.when(j + ahead < chunks)
        def _():
            start_grads(j + ahead, offsets)

        own_grads(j).wait()
        load_momentum(j).wait()
        right_high, right_low = split(right_ref[...])
        right_both = jnp.concatenate([right_high, right_low], axis=0)
        left = left_ref[...]
        for t in range(2):
            part = pl.ds(t * half, half)
            gradient = dot_nn(acts_t[part, :], grads_all[j])
            value = DECAY * residual_ref[j, part, :] + gradient
            residual_ref[j, part, :] = value
            high, low = split(value)
            both = dot_nt(high, right_both)
            done = both[:, :lanes] + both[:, lanes:] + dot_nt(low, right_high)
            coeffs[j, pl.ds(t * bands, bands), :] = jnp.sum(
                done.reshape(bands, GROUP, lanes) * left[None], axis=1
            )
        for q in range(1, reps):
            send_coeffs(q, j).start()
        for t in range(2):
            part = pl.ds(t * half, half)
            values = coeffs[j, pl.ds(t * bands, bands), :]
            residual_ref[j, part, :] = residual_ref[j, part, :] - decode(values, left, right_high, right_low)

        @pl.when(j > 0)
        def _():
            finish(j - 1, True)

        return carry

    lax.fori_loop(0, chunks, chunk, 0)

    def drain(j, carry):
        for o in range(1, shards):
            send_grads(o, j).wait_send()
        return carry

    lax.fori_loop(0, chunks, drain, 0)
    for c in direct:
        send_direct(2 * c).wait_send()
    for o in range(0, shards, 2):
        send_sibling(o).wait_send()
    if square:
        send_across(2).wait_send()
        send_across(4).wait_send()
    finish(chunks - 1, False)
    for j in range(chunks):
        for q in range(1, reps):
            send_coeffs(q, j).wait_send()


def store_kernel(
    residual_ref, update_ref, total_ref, right_ref, left_ref, residual_out, update_out, last, residual_sem, update_sem
):
    chunks, rows, _ = residual_ref.shape

    def store(source, target, sem, j):
        return pltpu.make_async_copy(source, target.at[:, pl.ds(j * WIDTH, WIDTH)], sem.at[j])

    copies = [store(update_ref.at[j], update_out, update_sem, j) for j in range(chunks - 1)]
    copies += [store(residual_ref.at[j], residual_out.at[0], residual_sem, j) for j in range(chunks)]
    for copy in copies:
        copy.start()
    right_high, right_low = split(right_ref[...])
    last[...] = decode(total_ref[...], left_ref[...], right_high, right_low).astype(jnp.bfloat16)
    copies.append(store(last, update_out, update_sem, chunks - 1))
    copies[-1].start()
    for copy in copies:
        copy.wait()


def on_device(shards, reps, hidden_acts, out_grads, momentum, kept):
    tok, rows = hidden_acts.shape
    columns = momentum.shape[2]
    chunks = columns // WIDTH
    kept_count = kept.shape[0]
    tiles = WIDTH // GROUP
    lanes = tiles * kept_count
    bands = rows // GROUP
    cosines = cosine_matrix(GROUP)
    table = np.concatenate(
        [np.tile(cosines, (1, tiles)), cosines.T, np.zeros((GROUP, 128 - GROUP), np.float32)], axis=1
    )
    f32 = jnp.float32
    hbm = pl.BlockSpec(memory_space=pltpu.HBM)
    vmem = pl.BlockSpec(memory_space=pltpu.VMEM)
    in_hbm = functools.partial(pltpu.with_memory_space_constraint, memory_space=pltpu.HBM)
    kept_parts = pl.pallas_call(
        functools.partial(exchange_kernel, shards, reps, chunks, kept_count),
        out_shape=(
            jax.ShapeDtypeStruct((chunks, rows, WIDTH), f32),
            jax.ShapeDtypeStruct((chunks, rows, WIDTH), jnp.bfloat16),
            jax.ShapeDtypeStruct((bands, lanes), f32),
            jax.ShapeDtypeStruct((lanes, WIDTH), f32),
            jax.ShapeDtypeStruct((GROUP, lanes), f32),
        ),
        in_specs=[hbm] * 5,
        out_specs=(vmem,) * 5,
        scratch_shapes=[
            pltpu.SMEM((kept_count,), jnp.int32),
            pltpu.VMEM(table.shape, f32),
            pltpu.VMEM((tok, rows), jnp.bfloat16),
            pltpu.VMEM((rows, shards * tok), jnp.bfloat16),
            pltpu.VMEM((chunks, shards * tok, WIDTH), jnp.bfloat16),
            pltpu.VMEM((chunks, bands, lanes), f32),
            pltpu.VMEM((chunks, reps, bands, lanes), f32),
            pltpu.SemaphoreType.DMA((shards + 1,)),
            pltpu.SemaphoreType.DMA((shards + 1,)),
            pltpu.SemaphoreType.DMA((chunks, shards)),
            pltpu.SemaphoreType.DMA((chunks, shards)),
            pltpu.SemaphoreType.DMA((chunks, reps)),
            pltpu.SemaphoreType.DMA((chunks, reps)),
            pltpu.SemaphoreType.DMA,
            pltpu.SemaphoreType.DMA,
            pltpu.SemaphoreType.DMA,
            pltpu.SemaphoreType.DMA((chunks,)),
            pltpu.SemaphoreType.DMA((chunks,)),
        ],
        compiler_params=pltpu.CompilerParams(
            collective_id=0, has_side_effects=True, vmem_limit_bytes=40 * 2**20
        ),
        name="exchange",
    )(*(in_hbm(x) for x in (kept, jnp.asarray(table), hidden_acts, out_grads, momentum)))
    return pl.pallas_call(
        store_kernel,
        out_shape=(
            jax.ShapeDtypeStruct((1, rows, columns), f32),
            jax.ShapeDtypeStruct((rows, columns), jnp.bfloat16),
        ),
        in_specs=[vmem] * 5,
        out_specs=(hbm, hbm),
        scratch_shapes=[
            pltpu.VMEM((rows, WIDTH), jnp.bfloat16),
            pltpu.SemaphoreType.DMA((chunks,)),
            pltpu.SemaphoreType.DMA((chunks,)),
        ],
        compiler_params=pltpu.CompilerParams(vmem_limit_bytes=24 * 2**20),
        name="store",
    )(*kept_parts)


def solution(mesh):
    placed = (P(("rep", "shard"), None), P(("rep", "shard"), None), P("rep", None, "shard"), P())
    return jax.shard_map(
        functools.partial(on_device, mesh.shape["shard"], mesh.shape["rep"]),
        mesh=mesh,
        in_specs=placed,
        out_specs=(P("rep", None, "shard"), P(None, "shard")),
        check_vma=False,
    )
```

```python
import functools
import math

import jax
import jax.numpy as jnp
import numpy as np
from jax import lax
from jax.experimental import pallas as pl
from jax.experimental.pallas import tpu as pltpu
from jax.sharding import PartitionSpec as P

GROUP = 64
WIDTH = 256
DECAY = 0.9
MESH = pl.DeviceIdType.MESH


def cosine_matrix(length):
    frequency = np.arange(length, dtype=np.float64)[:, None]
    position = np.arange(length, dtype=np.float64)[None, :]
    cosines = np.cos(math.pi * (2.0 * position + 1.0) * frequency / (2.0 * length)) * math.sqrt(2.0 / length)
    return (cosines * np.where(frequency == 0.0, math.sqrt(0.5), 1.0)).astype(np.float32)


def flip(index, bits):
    out = index
    power = 1
    while power <= bits:
        if bits & power:
            out = out + power - 2 * power * ((index // power) % 2)
        power *= 2
    return out


def split(x):
    high = x.astype(jnp.bfloat16)
    return high, (x - high.astype(jnp.float32)).astype(jnp.bfloat16)


def dot_nt(a, b):
    return lax.dot_general(a, b, (((1,), (1,)), ((), ())), preferred_element_type=jnp.float32)


def dot_nn(a, b):
    return lax.dot_general(a, b, (((1,), (0,)), ((), ())), preferred_element_type=jnp.float32)


def decode(values, left, right_high, right_low):
    bands, lanes = values.shape
    dense = (values[:, None, :] * left[None]).reshape(bands * GROUP, lanes)
    high, low = split(dense)
    twice = jnp.concatenate([right_high, right_high], axis=0)
    return dot_nn(jnp.concatenate([high, low], axis=1), twice) + dot_nn(high, right_low)


def exchange_kernel(
    shards, reps, chunks, kept_count,
    kept_hbm, table_hbm, acts_ref, grads_ref, momentum_ref,
    residual_ref, update_ref, total_ref, right_ref, left_ref,
    kept_ref, table, acts_all, acts_t, grads_all, coeffs, gathered,
    acts_send, acts_recv, grads_send, grads_recv, rep_send, rep_recv,
    local_kept, local_table, local_acts, local_grads, local_mom,
):
    rep = lax.axis_index("rep")
    me = lax.axis_index("shard")
    core = me % 2
    tok, rows = acts_ref.shape
    columns = chunks * WIDTH
    tiles = WIDTH // GROUP
    lanes = tiles * kept_count
    chips = shards // 2
    square = chips == 4
    offsets = sorted(range(1, chips), key=lambda c: c == 2)

    load_acts = pltpu.make_async_copy(acts_ref, acts_all.at[pl.ds(0, tok), :], local_acts)
    load_kept = pltpu.make_async_copy(kept_hbm, kept_ref, local_kept)
    load_table = pltpu.make_async_copy(table_hbm, table, local_table)
    load_acts.start()

    barrier = pltpu.get_barrier_semaphore()
    for o in range(1, shards):
        pl.semaphore_signal(barrier, inc=1, device_id=(rep, flip(me, o)), device_id_type=MESH)
    for q in range(1, reps):
        pl.semaphore_signal(barrier, inc=1, device_id=(flip(rep, q), me), device_id_type=MESH)
    load_kept.start()
    load_table.start()

    def own_grads(j):
        return pltpu.make_async_copy(
            grads_ref.at[:, pl.ds(pl.multiple_of(me * columns + j * WIDTH, WIDTH), WIDTH)],
            grads_all.at[j, pl.ds(0, tok), :],
            local_grads.at[j],
        )

    def load_momentum(j):
        return pltpu.make_async_copy(
            momentum_ref.at[0, :, pl.ds(pl.multiple_of(j * WIDTH, WIDTH), WIDTH)],
            residual_ref.at[j],
            local_mom.at[j],
        )

    def send_grads(o, j):
        peer = flip(me, o)
        return pltpu.make_async_remote_copy(
            src_ref=grads_ref.at[:, pl.ds(pl.multiple_of(peer * columns + j * WIDTH, WIDTH), WIDTH)],
            dst_ref=grads_all.at[j, pl.ds(o * tok, tok), :],
            send_sem=grads_send.at[j, o],
            recv_sem=grads_recv.at[j, o],
            device_id=(rep, peer),
            device_id_type=MESH,
        )

    def start_grads(j, some):
        for own, order in ((0, some), (1, some[::-1])):
            @pl.when(core == own)
            def _():
                for c in order:
                    send_grads(2 * c, j).start()
                    send_grads(2 * c + 1, j).start()
        if 1 in some:
            send_grads(1, j).start()

    def acts_copy(source, slot, bits, low, count, sem):
        own = acts_ref if source == 0 else acts_all.at[pl.ds(source * tok, tok), :]
        return pltpu.make_async_remote_copy(
            src_ref=own.at[pl.ds(low, count), :],
            dst_ref=acts_all.at[pl.ds(slot * tok + low, count), :],
            send_sem=acts_send.at[sem],
            recv_sem=acts_recv.at[sem],
            device_id=(rep, flip(me, bits)),
            device_id_type=MESH,
        )

    def send_direct(o):
        return acts_copy(0, o, o, 0, tok, o)

    def send_sibling(o):
        return acts_copy(o, o + 1, 1, 0, tok, o + 1)

    def turn(o):
        acts_t[:, pl.ds(o * tok, tok)] = acts_all[pl.ds(o * tok, tok), :].T

    def send_across(bits):
        if bits == 2:
            return acts_copy(4, 6, 2, tok // 2, tok // 2, shards)
        return acts_copy(2, 6, 4, 0, tok // 2, 6)

    def send_coeffs(q, j):
        return pltpu.make_async_remote_copy(
            src_ref=coeffs.at[j],
            dst_ref=gathered.at[j, q],
            send_sem=rep_send.at[j, q],
            recv_sem=rep_recv.at[j, q],
            device_id=(flip(rep, q), me),
            device_id_type=MESH,
        )

    direct = [c for c in offsets if not (square and c == 3)]
    pl.semaphore_wait(barrier, shards - 1 + reps - 1)
    for own, order in ((0, direct), (1, direct[::-1])):
        @pl.when(core == own)
        def _():
            for c in order:
                send_direct(2 * c).start()
    send_sibling(0).start()
    for j in range(min(2, chunks)):
        start_grads(j, offsets)
    for j in range(chunks):
        own_grads(j).start()
        load_momentum(j).start()

    load_kept.wait()
    load_table.wait()
    row = lax.broadcasted_iota(jnp.int32, (lanes, GROUP), 0) % kept_count
    freq_v = lax.broadcasted_iota(jnp.int32, (lanes, GROUP), 1)
    lane = lax.broadcasted_iota(jnp.int32, (GROUP, lanes), 1) % kept_count
    freq_u = lax.broadcasted_iota(jnp.int32, (GROUP, lanes), 0)
    hot_v = jnp.zeros((lanes, GROUP), jnp.float32)
    hot_u = jnp.zeros((GROUP, lanes), jnp.float32)
    for k in range(kept_count):
        index = kept_ref[k]
        hot_v = jnp.where((row == k) & (freq_v == index % GROUP), 1.0, hot_v)
        hot_u = jnp.where((lane == k) & (freq_u == index // GROUP), 1.0, hot_u)
    right = jnp.dot(
        hot_v, table[:, :WIDTH], precision=lax.Precision.HIGHEST, preferred_element_type=jnp.float32
    )
    same_tile = (
        lax.broadcasted_iota(jnp.int32, (lanes, WIDTH), 0) // kept_count
        == lax.broadcasted_iota(jnp.int32, (lanes, WIDTH), 1) // GROUP
    )
    right_ref[...] = jnp.where(same_tile, right, 0.0)
    left_ref[...] = jnp.dot(
        table[:, WIDTH:WIDTH + GROUP], hot_u, precision=lax.Precision.HIGHEST, preferred_element_type=jnp.float32
    )

    load_acts.wait()
    turn(0)
    for own, order in ((0, direct), (1, direct[::-1])):
        @pl.when(core == own)
        def _():
            for c in order:
                send_direct(2 * c).wait_recv()
                if square:
                    send_across(6 - 2 * c).start()
                send_sibling(2 * c).start()
    ahead = min(4, chunks)
    for j in range(2, min(3, chunks)):
        start_grads(j, offsets)
    for c in direct:
        turn(2 * c)
    for o in range(0, shards, 2):
        if not (square and o == 6):
            send_sibling(o).wait_recv()
            turn(o + 1)
    if square:
        send_across(4).wait_recv()
        send_across(2).wait_recv()
        send_sibling(6).start()
    for j in range(3, ahead):
        start_grads(j, offsets)
    if square:
        turn(6)
        send_sibling(6).wait_recv()
        turn(7)

    half = rows // 2
    bands = half // GROUP

    def finish(j, with_update):
        for q in range(1, reps):
            send_coeffs(q, j).wait_recv()
        terms = [coeffs[j]] + [gathered[j, q] for q in range(1, reps)]
        while len(terms) > 1:
            terms = [terms[i] + terms[i + 1] for i in range(0, len(terms), 2)]
        total_ref[...] = terms[0]
        if with_update:
            right_high, right_low = split(right_ref[...])
            for t in range(2):
                values = total_ref[pl.ds(t * bands, bands), :]
                update_ref[j, pl.ds(t * half, half), :] = decode(
                    values, left_ref[...], right_high, right_low
                ).astype(jnp.bfloat16)

    def chunk(j, carry):
        for o in range(1, shards):
            send_grads(o, j).wait_recv()

        @pl.when(j + ahead < chunks)
        def _():
            start_grads(j + ahead, offsets)

        own_grads(j).wait()
        load_momentum(j).wait()
        right_high, right_low = split(right_ref[...])
        right_both = jnp.concatenate([right_high, right_low], axis=0)
        left = left_ref[...]
        for t in range(2):
            part = pl.ds(t * half, half)
            gradient = dot_nn(acts_t[part, :], grads_all[j])
            value = DECAY * residual_ref[j, part, :] + gradient
            residual_ref[j, part, :] = value
            high, low = split(value)
            both = dot_nt(high, right_both)
            done = both[:, :lanes] + both[:, lanes:] + dot_nt(low, right_high)
            coeffs[j, pl.ds(t * bands, bands), :] = jnp.sum(
                done.reshape(bands, GROUP, lanes) * left[None], axis=1
            )
        for q in range(1, reps):
            send_coeffs(q, j).start()
        for t in range(2):
            part = pl.ds(t * half, half)
            values = coeffs[j, pl.ds(t * bands, bands), :]
            residual_ref[j, part, :] = residual_ref[j, part, :] - decode(values, left, right_high, right_low)

        @pl.when(j > 0)
        def _():
            finish(j - 1, True)

        return carry

    lax.fori_loop(0, chunks, chunk, 0)

    def drain(j, carry):
        for o in range(1, shards):
            send_grads(o, j).wait_send()
        return carry

    lax.fori_loop(0, chunks, drain, 0)
    for c in direct:
        send_direct(2 * c).wait_send()
    for o in range(0, shards, 2):
        send_sibling(o).wait_send()
    if square:
        send_across(2).wait_send()
        send_across(4).wait_send()
    finish(chunks - 1, False)
    for j in range(chunks):
        for q in range(1, reps):
            send_coeffs(q, j).wait_send()


def store_kernel(
    residual_ref, update_ref, total_ref, right_ref, left_ref, residual_out, update_out, last, residual_sem, update_sem
):
    chunks, rows, _ = residual_ref.shape

    def store(source, target, sem, j):
        return pltpu.make_async_copy(source, target.at[:, pl.ds(j * WIDTH, WIDTH)], sem.at[j])

    copies = [store(update_ref.at[j], update_out, update_sem, j) for j in range(chunks - 1)]
    copies += [store(residual_ref.at[j], residual_out.at[0], residual_sem, j) for j in range(chunks)]
    for copy in copies:
        copy.start()
    right_high, right_low = split(right_ref[...])
    last[...] = decode(total_ref[...], left_ref[...], right_high, right_low).astype(jnp.bfloat16)
    copies.append(store(last, update_out, update_sem, chunks - 1))
    copies[-1].start()
    for copy in copies:
        copy.wait()


def on_device(shards, reps, hidden_acts, out_grads, momentum, kept):
    tok, rows = hidden_acts.shape
    columns = momentum.shape[2]
    chunks = columns // WIDTH
    kept_count = kept.shape[0]
    tiles = WIDTH // GROUP
    lanes = tiles * kept_count
    bands = rows // GROUP
    cosines = cosine_matrix(GROUP)
    table = np.concatenate(
        [np.tile(cosines, (1, tiles)), cosines.T, np.zeros((GROUP, 128 - GROUP), np.float32)], axis=1
    )
    f32 = jnp.float32
    hbm = pl.BlockSpec(memory_space=pltpu.HBM)
    vmem = pl.BlockSpec(memory_space=pltpu.VMEM)
    in_hbm = functools.partial(pltpu.with_memory_space_constraint, memory_space=pltpu.HBM)
    kept_parts = pl.pallas_call(
        functools.partial(exchange_kernel, shards, reps, chunks, kept_count),
        out_shape=(
            jax.ShapeDtypeStruct((chunks, rows, WIDTH), f32),
            jax.ShapeDtypeStruct((chunks, rows, WIDTH), jnp.bfloat16),
            jax.ShapeDtypeStruct((bands, lanes), f32),
            jax.ShapeDtypeStruct((lanes, WIDTH), f32),
            jax.ShapeDtypeStruct((GROUP, lanes), f32),
        ),
        in_specs=[hbm] * 5,
        out_specs=(vmem,) * 5,
        scratch_shapes=[
            pltpu.SMEM((kept_count,), jnp.int32),
            pltpu.VMEM(table.shape, f32),
            pltpu.VMEM((shards * tok, rows), jnp.bfloat16),
            pltpu.VMEM((rows, shards * tok), jnp.bfloat16),
            pltpu.VMEM((chunks, shards * tok, WIDTH), jnp.bfloat16),
            pltpu.VMEM((chunks, bands, lanes), f32),
            pltpu.VMEM((chunks, reps, bands, lanes), f32),
            pltpu.SemaphoreType.DMA((shards + 1,)),
            pltpu.SemaphoreType.DMA((shards + 1,)),
            pltpu.SemaphoreType.DMA((chunks, shards)),
            pltpu.SemaphoreType.DMA((chunks, shards)),
            pltpu.SemaphoreType.DMA((chunks, reps)),
            pltpu.SemaphoreType.DMA((chunks, reps)),
            pltpu.SemaphoreType.DMA,
            pltpu.SemaphoreType.DMA,
            pltpu.SemaphoreType.DMA,
            pltpu.SemaphoreType.DMA((chunks,)),
            pltpu.SemaphoreType.DMA((chunks,)),
        ],
        compiler_params=pltpu.CompilerParams(
            collective_id=0, has_side_effects=True, vmem_limit_bytes=40 * 2**20
        ),
        name="exchange",
    )(*(in_hbm(x) for x in (kept, jnp.asarray(table), hidden_acts, out_grads, momentum)))
    return pl.pallas_call(
        store_kernel,
        out_shape=(
            jax.ShapeDtypeStruct((1, rows, columns), f32),
            jax.ShapeDtypeStruct((rows, columns), jnp.bfloat16),
        ),
        in_specs=[vmem] * 5,
        out_specs=(hbm, hbm),
        scratch_shapes=[
            pltpu.VMEM((rows, WIDTH), jnp.bfloat16),
            pltpu.SemaphoreType.DMA((chunks,)),
            pltpu.SemaphoreType.DMA((chunks,)),
        ],
        compiler_params=pltpu.CompilerParams(vmem_limit_bytes=24 * 2**20),
        name="store",
    )(*kept_parts)


def solution(mesh):
    placed = (P(("rep", "shard"), None), P(("rep", "shard"), None), P("rep", None, "shard"), P())
    return jax.shard_map(
        functools.partial(on_device, mesh.shape["shard"], mesh.shape["rep"]),
        mesh=mesh,
        in_specs=placed,
        out_specs=(P("rep", None, "shard"), P(None, "shard")),
        check_vma=False,
    )
```

```python
import functools
import math

import jax
import jax.numpy as jnp
import numpy as np
from jax import lax
from jax.experimental import pallas as pl
from jax.experimental.pallas import tpu as pltpu
from jax.sharding import PartitionSpec as P

GROUP = 64
WIDTH = 256
DECAY = 0.9
MESH = pl.DeviceIdType.MESH


def cosine_matrix(length):
    frequency = np.arange(length, dtype=np.float64)[:, None]
    position = np.arange(length, dtype=np.float64)[None, :]
    cosines = np.cos(math.pi * (2.0 * position + 1.0) * frequency / (2.0 * length)) * math.sqrt(2.0 / length)
    return (cosines * np.where(frequency == 0.0, math.sqrt(0.5), 1.0)).astype(np.float32)


def flip(index, bits):
    out = index
    power = 1
    while power <= bits:
        if bits & power:
            out = out + power - 2 * power * ((index // power) % 2)
        power *= 2
    return out


def split(x):
    high = x.astype(jnp.bfloat16)
    return high, (x - high.astype(jnp.float32)).astype(jnp.bfloat16)


def dot_nt(a, b):
    return lax.dot_general(a, b, (((1,), (1,)), ((), ())), preferred_element_type=jnp.float32)


def dot_nn(a, b):
    return lax.dot_general(a, b, (((1,), (0,)), ((), ())), preferred_element_type=jnp.float32)


def decode(values, left, right_high, right_low):
    bands, lanes = values.shape
    dense = (values[:, None, :] * left[None]).reshape(bands * GROUP, lanes)
    high, low = split(dense)
    twice = jnp.concatenate([right_high, right_high], axis=0)
    return dot_nn(jnp.concatenate([high, low], axis=1), twice) + dot_nn(high, right_low)


def exchange_kernel(
    shards, reps, chunks, kept_count,
    kept_hbm, table_hbm, acts_ref, grads_ref, momentum_ref,
    residual_ref, update_ref, total_ref, right_ref, left_ref,
    kept_ref, table, acts_all, acts_t, grads_all, coeffs, gathered,
    acts_send, acts_recv, grads_send, grads_recv, rep_send, rep_recv,
    local_kept, local_table, local_acts, local_grads, local_mom, transit, transit_send, transit_recv,
):
    rep = lax.axis_index("rep")
    me = lax.axis_index("shard")
    core = me % 2
    tok, rows = acts_ref.shape
    columns = chunks * WIDTH
    tiles = WIDTH // GROUP
    lanes = tiles * kept_count
    chips = shards // 2
    square = chips == 4
    direct = [c for c in range(1, chips) if not (square and c == 3)]
    straight = [1] + [2 * c + b for c in direct for b in range(2)]

    load_acts = pltpu.make_async_copy(acts_ref, acts_all.at[pl.ds(0, tok), :], local_acts)
    load_kept = pltpu.make_async_copy(kept_hbm, kept_ref, local_kept)
    load_table = pltpu.make_async_copy(table_hbm, table, local_table)
    load_acts.start()

    barrier = pltpu.get_barrier_semaphore()
    for o in range(1, shards):
        pl.semaphore_signal(barrier, inc=1, device_id=(rep, flip(me, o)), device_id_type=MESH)
    for q in range(1, reps):
        pl.semaphore_signal(barrier, inc=1, device_id=(flip(rep, q), me), device_id_type=MESH)
    load_kept.start()
    load_table.start()

    def own_grads(j):
        return pltpu.make_async_copy(
            grads_ref.at[:, pl.ds(pl.multiple_of(me * columns + j * WIDTH, WIDTH), WIDTH)],
            grads_all.at[j, pl.ds(0, tok), :],
            local_grads.at[j],
        )

    def load_momentum(j):
        return pltpu.make_async_copy(
            momentum_ref.at[0, :, pl.ds(pl.multiple_of(j * WIDTH, WIDTH), WIDTH)],
            residual_ref.at[j],
            local_mom.at[j],
        )

    def send_grads(o, j):
        peer = flip(me, o)
        return pltpu.make_async_remote_copy(
            src_ref=grads_ref.at[:, pl.ds(pl.multiple_of(peer * columns + j * WIDTH, WIDTH), WIDTH)],
            dst_ref=grads_all.at[j, pl.ds(o * tok, tok), :],
            send_sem=grads_send.at[j, o],
            recv_sem=grads_recv.at[j, o],
            device_id=(rep, peer),
            device_id_type=MESH,
        )

    def start_grads(j, some):
        for own, order in ((0, some), (1, some[::-1])):
            @pl.when(core == own)
            def _():
                if square:
                    for c in order:
                        for b in range(2):
                            first_hop(c, b, j).start()
                for c in order:
                    send_grads(2 * c, j).start()
                    send_grads(2 * c + 1, j).start()
        send_grads(1, j).start()

    def first_hop(c, b, j):
        peer = flip(me, 6 + b)
        column = pl.multiple_of(peer * columns + j * WIDTH, WIDTH)
        return pltpu.make_async_remote_copy(
            src_ref=grads_ref.at[pl.ds((c - 1) * (tok // 2), tok // 2), pl.ds(column, WIDTH)],
            dst_ref=transit.at[j, c - 1, b],
            send_sem=transit_send.at[j, c - 1, b],
            recv_sem=transit_recv.at[j, c - 1, b],
            device_id=(rep, flip(me, 2 * c)),
            device_id_type=MESH,
        )

    def second_hop(c, b, j):
        return pltpu.make_async_remote_copy(
            src_ref=transit.at[j, c - 1, b],
            dst_ref=grads_all.at[j, pl.ds((6 + b) * tok + (c - 1) * (tok // 2), tok // 2), :],
            send_sem=grads_send.at[j, 6 + b + 2 * (c - 1)],
            recv_sem=grads_recv.at[j, 6 + b + 2 * (c - 1)],
            device_id=(rep, flip(me, 6 - 2 * c + b)),
            device_id_type=MESH,
        )

    def hand_on(j):
        for own, order in ((0, direct), (1, direct[::-1])):
            @pl.when(core == own)
            def _():
                for c in order:
                    for b in range(2):
                        first_hop(c, b, j).wait_recv()
                        second_hop(c, b, j).start()

    hops = [(c, b) for c in (1, 2) for b in range(2)] if square else []

    def acts_copy(source, slot, bits, low, count, sem):
        own = acts_ref if source == 0 else acts_all.at[pl.ds(source * tok, tok), :]
        return pltpu.make_async_remote_copy(
            src_ref=own.at[pl.ds(low, count), :],
            dst_ref=acts_all.at[pl.ds(slot * tok + low, count), :],
            send_sem=acts_send.at[sem],
            recv_sem=acts_recv.at[sem],
            device_id=(rep, flip(me, bits)),
            device_id_type=MESH,
        )

    def send_direct(o):
        return acts_copy(0, o, o, 0, tok, o)

    def send_sibling(o):
        return acts_copy(o, o + 1, 1, 0, tok, o + 1)

    def turn(o):
        acts_t[:, pl.ds(o * tok, tok)] = acts_all[pl.ds(o * tok, tok), :].T

    def send_across(bits):
        if bits == 2:
            return acts_copy(4, 6, 2, tok // 2, tok // 2, shards)
        return acts_copy(2, 6, 4, 0, tok // 2, 6)

    def send_coeffs(q, j):
        return pltpu.make_async_remote_copy(
            src_ref=coeffs.at[j],
            dst_ref=gathered.at[j, q],
            send_sem=rep_send.at[j, q],
            recv_sem=rep_recv.at[j, q],
            device_id=(flip(rep, q), me),
            device_id_type=MESH,
        )

    pl.semaphore_wait(barrier, shards - 1 + reps - 1)
    for own, order in ((0, direct), (1, direct[::-1])):
        @pl.when(core == own)
        def _():
            for c in order:
                send_direct(2 * c).start()
    send_sibling(0).start()
    for j in range(min(2, chunks)):
        start_grads(j, direct)
    for j in range(chunks):
        own_grads(j).start()
        load_momentum(j).start()

    load_kept.wait()
    load_table.wait()
    row = lax.broadcasted_iota(jnp.int32, (lanes, GROUP), 0) % kept_count
    freq_v = lax.broadcasted_iota(jnp.int32, (lanes, GROUP), 1)
    lane = lax.broadcasted_iota(jnp.int32, (GROUP, lanes), 1) % kept_count
    freq_u = lax.broadcasted_iota(jnp.int32, (GROUP, lanes), 0)
    hot_v = jnp.zeros((lanes, GROUP), jnp.float32)
    hot_u = jnp.zeros((GROUP, lanes), jnp.float32)
    for k in range(kept_count):
        index = kept_ref[k]
        hot_v = jnp.where((row == k) & (freq_v == index % GROUP), 1.0, hot_v)
        hot_u = jnp.where((lane == k) & (freq_u == index // GROUP), 1.0, hot_u)
    right = jnp.dot(
        hot_v, table[:, :WIDTH], precision=lax.Precision.HIGHEST, preferred_element_type=jnp.float32
    )
    same_tile = (
        lax.broadcasted_iota(jnp.int32, (lanes, WIDTH), 0) // kept_count
        == lax.broadcasted_iota(jnp.int32, (lanes, WIDTH), 1) // GROUP
    )
    right_ref[...] = jnp.where(same_tile, right, 0.0)
    left_ref[...] = jnp.dot(
        table[:, WIDTH:WIDTH + GROUP], hot_u, precision=lax.Precision.HIGHEST, preferred_element_type=jnp.float32
    )

    load_acts.wait()
    turn(0)
    for own, order in ((0, direct), (1, direct[::-1])):
        @pl.when(core == own)
        def _():
            for c in order:
                send_direct(2 * c).wait_recv()
                if square:
                    send_across(6 - 2 * c).start()
                send_sibling(2 * c).start()
    ahead = min(4, chunks)
    for j in range(2, min(3, chunks)):
        start_grads(j, direct)
    for c in direct:
        turn(2 * c)
    for o in range(0, shards, 2):
        if not (square and o == 6):
            send_sibling(o).wait_recv()
            turn(o + 1)
    if square:
        send_across(4).wait_recv()
        send_across(2).wait_recv()
        send_sibling(6).start()
    for j in range(3, ahead):
        start_grads(j, direct)
    if square:
        hand_on(0)
        turn(6)
        send_sibling(6).wait_recv()
        turn(7)

    half = rows // 2
    bands = half // GROUP

    def finish(j, with_update):
        for q in range(1, reps):
            send_coeffs(q, j).wait_recv()
        terms = [coeffs[j]] + [gathered[j, q] for q in range(1, reps)]
        while len(terms) > 1:
            terms = [terms[i] + terms[i + 1] for i in range(0, len(terms), 2)]
        total_ref[...] = terms[0]
        if with_update:
            right_high, right_low = split(right_ref[...])
            for t in range(2):
                values = total_ref[pl.ds(t * bands, bands), :]
                update_ref[j, pl.ds(t * half, half), :] = decode(
                    values, left_ref[...], right_high, right_low
                ).astype(jnp.bfloat16)

    def chunk(j, carry):
        if square:
            @pl.when(j + 1 < chunks)
            def _():
                hand_on(j + 1)

        for o in straight:
            send_grads(o, j).wait_recv()
        for c, b in hops:
            second_hop(c, b, j).wait_recv()

        @pl.when(j + ahead < chunks)
        def _():
            start_grads(j + ahead, direct)

        own_grads(j).wait()
        load_momentum(j).wait()
        right_high, right_low = split(right_ref[...])
        right_both = jnp.concatenate([right_high, right_low], axis=0)
        left = left_ref[...]
        for t in range(2):
            part = pl.ds(t * half, half)
            gradient = dot_nn(acts_t[part, :], grads_all[j])
            value = DECAY * residual_ref[j, part, :] + gradient
            residual_ref[j, part, :] = value
            high, low = split(value)
            both = dot_nt(high, right_both)
            done = both[:, :lanes] + both[:, lanes:] + dot_nt(low, right_high)
            coeffs[j, pl.ds(t * bands, bands), :] = jnp.sum(
                done.reshape(bands, GROUP, lanes) * left[None], axis=1
            )
        for q in range(1, reps):
            send_coeffs(q, j).start()
        for t in range(2):
            part = pl.ds(t * half, half)
            values = coeffs[j, pl.ds(t * bands, bands), :]
            residual_ref[j, part, :] = residual_ref[j, part, :] - decode(values, left, right_high, right_low)

        @pl.when(j > 0)
        def _():
            finish(j - 1, True)

        return carry

    lax.fori_loop(0, chunks, chunk, 0)

    def drain(j, carry):
        for o in straight:
            send_grads(o, j).wait_send()
        for c, b in hops:
            first_hop(c, b, j).wait_send()
            second_hop(c, b, j).wait_send()
        return carry

    lax.fori_loop(0, chunks, drain, 0)
    for c in direct:
        send_direct(2 * c).wait_send()
    for o in range(0, shards, 2):
        send_sibling(o).wait_send()
    if square:
        send_across(2).wait_send()
        send_across(4).wait_send()
    finish(chunks - 1, False)
    for j in range(chunks):
        for q in range(1, reps):
            send_coeffs(q, j).wait_send()


def store_kernel(
    residual_ref, update_ref, total_ref, right_ref, left_ref, residual_out, update_out, last, residual_sem, update_sem
):
    chunks, rows, _ = residual_ref.shape

    def store(source, target, sem, j):
        return pltpu.make_async_copy(source, target.at[:, pl.ds(j * WIDTH, WIDTH)], sem.at[j])

    copies = [store(update_ref.at[j], update_out, update_sem, j) for j in range(chunks - 1)]
    copies += [store(residual_ref.at[j], residual_out.at[0], residual_sem, j) for j in range(chunks)]
    for copy in copies:
        copy.start()
    right_high, right_low = split(right_ref[...])
    last[...] = decode(total_ref[...], left_ref[...], right_high, right_low).astype(jnp.bfloat16)
    copies.append(store(last, update_out, update_sem, chunks - 1))
    copies[-1].start()
    for copy in copies:
        copy.wait()


def on_device(shards, reps, hidden_acts, out_grads, momentum, kept):
    tok, rows = hidden_acts.shape
    columns = momentum.shape[2]
    chunks = columns // WIDTH
    kept_count = kept.shape[0]
    tiles = WIDTH // GROUP
    lanes = tiles * kept_count
    bands = rows // GROUP
    cosines = cosine_matrix(GROUP)
    table = np.concatenate(
        [np.tile(cosines, (1, tiles)), cosines.T, np.zeros((GROUP, 128 - GROUP), np.float32)], axis=1
    )
    f32 = jnp.float32
    hbm = pl.BlockSpec(memory_space=pltpu.HBM)
    vmem = pl.BlockSpec(memory_space=pltpu.VMEM)
    in_hbm = functools.partial(pltpu.with_memory_space_constraint, memory_space=pltpu.HBM)
    kept_parts = pl.pallas_call(
        functools.partial(exchange_kernel, shards, reps, chunks, kept_count),
        out_shape=(
            jax.ShapeDtypeStruct((chunks, rows, WIDTH), f32),
            jax.ShapeDtypeStruct((chunks, rows, WIDTH), jnp.bfloat16),
            jax.ShapeDtypeStruct((bands, lanes), f32),
            jax.ShapeDtypeStruct((lanes, WIDTH), f32),
            jax.ShapeDtypeStruct((GROUP, lanes), f32),
        ),
        in_specs=[hbm] * 5,
        out_specs=(vmem,) * 5,
        scratch_shapes=[
            pltpu.SMEM((kept_count,), jnp.int32),
            pltpu.VMEM(table.shape, f32),
            pltpu.VMEM((shards * tok, rows), jnp.bfloat16),
            pltpu.VMEM((rows, shards * tok), jnp.bfloat16),
            pltpu.VMEM((chunks, shards * tok, WIDTH), jnp.bfloat16),
            pltpu.VMEM((chunks, bands, lanes), f32),
            pltpu.VMEM((chunks, reps, bands, lanes), f32),
            pltpu.SemaphoreType.DMA((shards + 1,)),
            pltpu.SemaphoreType.DMA((shards + 1,)),
            pltpu.SemaphoreType.DMA((chunks, shards + 2)),
            pltpu.SemaphoreType.DMA((chunks, shards + 2)),
            pltpu.SemaphoreType.DMA((chunks, reps)),
            pltpu.SemaphoreType.DMA((chunks, reps)),
            pltpu.SemaphoreType.DMA,
            pltpu.SemaphoreType.DMA,
            pltpu.SemaphoreType.DMA,
            pltpu.SemaphoreType.DMA((chunks,)),
            pltpu.SemaphoreType.DMA((chunks,)),
            pltpu.VMEM((chunks, 2, 2, tok // 2, WIDTH), jnp.bfloat16),
            pltpu.SemaphoreType.DMA((chunks, 2, 2)),
            pltpu.SemaphoreType.DMA((chunks, 2, 2)),
        ],
        compiler_params=pltpu.CompilerParams(
            collective_id=0, has_side_effects=True, vmem_limit_bytes=40 * 2**20
        ),
        name="exchange",
    )(*(in_hbm(x) for x in (kept, jnp.asarray(table), hidden_acts, out_grads, momentum)))
    return pl.pallas_call(
        store_kernel,
        out_shape=(
            jax.ShapeDtypeStruct((1, rows, columns), f32),
            jax.ShapeDtypeStruct((rows, columns), jnp.bfloat16),
        ),
        in_specs=[vmem] * 5,
        out_specs=(hbm, hbm),
        scratch_shapes=[
            pltpu.VMEM((rows, WIDTH), jnp.bfloat16),
            pltpu.SemaphoreType.DMA((chunks,)),
            pltpu.SemaphoreType.DMA((chunks,)),
        ],
        compiler_params=pltpu.CompilerParams(vmem_limit_bytes=24 * 2**20),
        name="store",
    )(*kept_parts)


def solution(mesh):
    placed = (P(("rep", "shard"), None), P(("rep", "shard"), None), P("rep", None, "shard"), P())
    return jax.shard_map(
        functools.partial(on_device, mesh.shape["shard"], mesh.shape["rep"]),
        mesh=mesh,
        in_specs=placed,
        out_specs=(P("rep", None, "shard"), P(None, "shard")),
        check_vma=False,
    )
```

```python
import functools
import math

import jax
import jax.numpy as jnp
import numpy as np
from jax import lax
from jax.experimental import pallas as pl
from jax.experimental.pallas import tpu as pltpu
from jax.sharding import PartitionSpec as P

GROUP = 64
WIDTH = 256
SPAN = 512
DECAY = 0.9
MESH = pl.DeviceIdType.MESH


def cosine_matrix(length):
    frequency = np.arange(length, dtype=np.float64)[:, None]
    position = np.arange(length, dtype=np.float64)[None, :]
    cosines = np.cos(math.pi * (2.0 * position + 1.0) * frequency / (2.0 * length)) * math.sqrt(2.0 / length)
    return (cosines * np.where(frequency == 0.0, math.sqrt(0.5), 1.0)).astype(np.float32)


def flip(index, bits):
    out = index
    power = 1
    while power <= bits:
        if bits & power:
            out = out + power - 2 * power * ((index // power) % 2)
        power *= 2
    return out


def split(x):
    high = x.astype(jnp.bfloat16)
    return high, (x - high.astype(jnp.float32)).astype(jnp.bfloat16)


def dot_nt(a, b):
    return lax.dot_general(a, b, (((1,), (1,)), ((), ())), preferred_element_type=jnp.float32)


def dot_nn(a, b):
    return lax.dot_general(a, b, (((1,), (0,)), ((), ())), preferred_element_type=jnp.float32)


def decode(values, left, right_high, right_low):
    bands, lanes = values.shape
    dense = (values[:, None, :] * left[None]).reshape(bands * GROUP, lanes)
    high, low = split(dense)
    twice = jnp.concatenate([right_high, right_high], axis=0)
    return dot_nn(jnp.concatenate([high, low], axis=1), twice) + dot_nn(high, right_low)


def exchange_kernel(
    shards, reps, chunks, kept_count,
    kept_hbm, table_hbm, acts_ref, grads_ref, momentum_ref,
    residual_ref, update_ref, total_ref, right_ref, left_ref,
    kept_ref, table, acts_all, acts_t, grads_all, coeffs, gathered,
    acts_send, acts_recv, grads_send, grads_recv, rep_send, rep_recv,
    local_kept, local_table, local_acts, local_grads, local_mom,
):
    rep = lax.axis_index("rep")
    me = lax.axis_index("shard")
    core = me % 2
    tok, rows = acts_ref.shape
    columns = chunks * WIDTH
    span = min(SPAN, columns)
    parts = span // WIDTH
    spans = columns // span
    tiles = WIDTH // GROUP
    lanes = tiles * kept_count
    chips = shards // 2
    square = chips == 4
    offsets = sorted(range(1, chips), key=lambda c: c == 2)

    load_acts = pltpu.make_async_copy(acts_ref, acts_all.at[pl.ds(0, tok), :], local_acts)
    load_kept = pltpu.make_async_copy(kept_hbm, kept_ref, local_kept)
    load_table = pltpu.make_async_copy(table_hbm, table, local_table)
    load_acts.start()

    barrier = pltpu.get_barrier_semaphore()
    for o in range(1, shards):
        pl.semaphore_signal(barrier, inc=1, device_id=(rep, flip(me, o)), device_id_type=MESH)
    for q in range(1, reps):
        pl.semaphore_signal(barrier, inc=1, device_id=(flip(rep, q), me), device_id_type=MESH)
    load_kept.start()
    load_table.start()

    def own_grads(j):
        return pltpu.make_async_copy(
            grads_ref.at[:, pl.ds(pl.multiple_of(me * columns + j * span, span), span)],
            grads_all.at[j, pl.ds(0, tok), :],
            local_grads.at[j],
        )

    def load_momentum(j):
        return pltpu.make_async_copy(
            momentum_ref.at[0, :, pl.ds(pl.multiple_of(j * WIDTH, WIDTH), WIDTH)],
            residual_ref.at[j],
            local_mom.at[j],
        )

    def send_grads(o, j):
        peer = flip(me, o)
        return pltpu.make_async_remote_copy(
            src_ref=grads_ref.at[:, pl.ds(pl.multiple_of(peer * columns + j * span, span), span)],
            dst_ref=grads_all.at[j, pl.ds(o * tok, tok), :],
            send_sem=grads_send.at[j, o],
            recv_sem=grads_recv.at[j, o],
            device_id=(rep, peer),
            device_id_type=MESH,
        )

    def start_grads(j, some):
        for own, order in ((0, some), (1, some[::-1])):
            @pl.when(core == own)
            def _():
                for c in order:
                    send_grads(2 * c, j).start()
                    send_grads(2 * c + 1, j).start()
        if 1 in some:
            send_grads(1, j).start()

    def acts_copy(source, slot, bits, low, count, sem):
        own = acts_ref if source == 0 else acts_all.at[pl.ds(source * tok, tok), :]
        return pltpu.make_async_remote_copy(
            src_ref=own.at[pl.ds(low, count), :],
            dst_ref=acts_all.at[pl.ds(slot * tok + low, count), :],
            send_sem=acts_send.at[sem],
            recv_sem=acts_recv.at[sem],
            device_id=(rep, flip(me, bits)),
            device_id_type=MESH,
        )

    def send_direct(o):
        return acts_copy(0, o, o, 0, tok, o)

    def send_sibling(o):
        return acts_copy(o, o + 1, 1, 0, tok, o + 1)

    def turn(o):
        acts_t[:, pl.ds(o * tok, tok)] = acts_all[pl.ds(o * tok, tok), :].T

    def send_across(bits):
        if bits == 2:
            return acts_copy(4, 6, 2, tok // 2, tok // 2, shards)
        return acts_copy(2, 6, 4, 0, tok // 2, 6)

    def send_coeffs(q, j):
        return pltpu.make_async_remote_copy(
            src_ref=coeffs.at[j],
            dst_ref=gathered.at[j, q],
            send_sem=rep_send.at[j, q],
            recv_sem=rep_recv.at[j, q],
            device_id=(flip(rep, q), me),
            device_id_type=MESH,
        )

    direct = [c for c in offsets if not (square and c == 3)]
    pl.semaphore_wait(barrier, shards - 1 + reps - 1)
    for own, order in ((0, direct), (1, direct[::-1])):
        @pl.when(core == own)
        def _():
            for c in order:
                send_direct(2 * c).start()
    send_sibling(0).start()
    ahead = min(2, spans)
    start_grads(0, offsets)
    for j in range(spans):
        own_grads(j).start()
    for j in range(chunks):
        load_momentum(j).start()

    load_kept.wait()
    load_table.wait()
    row = lax.broadcasted_iota(jnp.int32, (lanes, GROUP), 0) % kept_count
    freq_v = lax.broadcasted_iota(jnp.int32, (lanes, GROUP), 1)
    lane = lax.broadcasted_iota(jnp.int32, (GROUP, lanes), 1) % kept_count
    freq_u = lax.broadcasted_iota(jnp.int32, (GROUP, lanes), 0)
    hot_v = jnp.zeros((lanes, GROUP), jnp.float32)
    hot_u = jnp.zeros((GROUP, lanes), jnp.float32)
    for k in range(kept_count):
        index = kept_ref[k]
        hot_v = jnp.where((row == k) & (freq_v == index % GROUP), 1.0, hot_v)
        hot_u = jnp.where((lane == k) & (freq_u == index // GROUP), 1.0, hot_u)
    right = jnp.dot(
        hot_v, table[:, :WIDTH], precision=lax.Precision.HIGHEST, preferred_element_type=jnp.float32
    )
    same_tile = (
        lax.broadcasted_iota(jnp.int32, (lanes, WIDTH), 0) // kept_count
        == lax.broadcasted_iota(jnp.int32, (lanes, WIDTH), 1) // GROUP
    )
    right_ref[...] = jnp.where(same_tile, right, 0.0)
    left_ref[...] = jnp.dot(
        table[:, WIDTH:WIDTH + GROUP], hot_u, precision=lax.Precision.HIGHEST, preferred_element_type=jnp.float32
    )

    load_acts.wait()
    turn(0)
    for own, order in ((0, direct), (1, direct[::-1])):
        @pl.when(core == own)
        def _():
            for c in order:
                send_direct(2 * c).wait_recv()
                if square:
                    send_across(6 - 2 * c).start()
                send_sibling(2 * c).start()
    for j in range(1, ahead):
        start_grads(j, offsets)
    for c in direct:
        turn(2 * c)
    for o in range(0, shards, 2):
        if not (square and o == 6):
            send_sibling(o).wait_recv()
            turn(o + 1)
    if square:
        send_across(4).wait_recv()
        send_across(2).wait_recv()
        send_sibling(6).start()
    if square:
        turn(6)
        send_sibling(6).wait_recv()
        turn(7)

    half = rows // 2
    bands = half // GROUP

    def add_replicas(j):
        for q in range(1, reps):
            send_coeffs(q, j).wait_recv()
        terms = [coeffs[j]] + [gathered[j, q] for q in range(1, reps)]
        while len(terms) > 1:
            terms = [terms[i] + terms[i + 1] for i in range(0, len(terms), 2)]
        return terms[0]

    def columns_span(i, carry):
        for o in range(1, shards):
            send_grads(o, i).wait_recv()

        @pl.when(i + ahead < spans)
        def _():
            start_grads(i + ahead, offsets)

        own_grads(i).wait()
        right_high, right_low = split(right_ref[...])
        right_both = jnp.concatenate([right_high, right_low], axis=0)
        left = left_ref[...]
        for p in range(parts):
            j = i * parts + p
            load_momentum(j).wait()
            for t in range(2):
                part = pl.ds(t * half, half)
                gradient = dot_nn(acts_t[part, :], grads_all[i, :, p * WIDTH:(p + 1) * WIDTH])
                value = DECAY * residual_ref[j, part, :] + gradient
                residual_ref[j, part, :] = value
                high, low = split(value)
                both = dot_nt(high, right_both)
                done = both[:, :lanes] + both[:, lanes:] + dot_nt(low, right_high)
                coeffs[j, pl.ds(t * bands, bands), :] = jnp.sum(
                    done.reshape(bands, GROUP, lanes) * left[None], axis=1
                )
            for q in range(1, reps):
                send_coeffs(q, j).start()
        for p in range(parts):
            j = i * parts + p
            for t in range(2):
                part = pl.ds(t * half, half)
                values = coeffs[j, pl.ds(t * bands, bands), :]
                residual_ref[j, part, :] = residual_ref[j, part, :] - decode(values, left, right_high, right_low)

        @pl.when(i > 0)
        def _():
            for p in range(parts):
                j = (i - 1) * parts + p
                total_ref[0] = add_replicas(j)
                for t in range(2):
                    values = total_ref[0, pl.ds(t * bands, bands), :]
                    update_ref[j, pl.ds(t * half, half), :] = decode(
                        values, left, right_high, right_low
                    ).astype(jnp.bfloat16)

        return carry

    lax.fori_loop(0, spans, columns_span, 0)

    def drain(j, carry):
        for o in range(1, shards):
            send_grads(o, j).wait_send()
        return carry

    lax.fori_loop(0, spans, drain, 0)
    for c in direct:
        send_direct(2 * c).wait_send()
    for o in range(0, shards, 2):
        send_sibling(o).wait_send()
    if square:
        send_across(2).wait_send()
        send_across(4).wait_send()
    for p in range(parts):
        total_ref[p] = add_replicas((spans - 1) * parts + p)
    for j in range(chunks):
        for q in range(1, reps):
            send_coeffs(q, j).wait_send()


def store_kernel(
    residual_ref, update_ref, total_ref, right_ref, left_ref, residual_out, update_out, last, residual_sem, update_sem
):
    chunks, rows, _ = residual_ref.shape

    def store(source, target, sem, j):
        return pltpu.make_async_copy(source, target.at[:, pl.ds(j * WIDTH, WIDTH)], sem.at[j])

    parts = total_ref.shape[0]
    copies = [store(residual_ref.at[j], residual_out.at[0], residual_sem, j) for j in range(chunks)]
    copies += [store(update_ref.at[j], update_out, update_sem, j) for j in range(chunks - parts)]
    for copy in copies:
        copy.start()
    right_high, right_low = split(right_ref[...])
    for p in range(parts):
        last[p] = decode(total_ref[p], left_ref[...], right_high, right_low).astype(jnp.bfloat16)
        copies.append(store(last.at[p], update_out, update_sem, chunks - parts + p))
        copies[-1].start()
    for copy in copies:
        copy.wait()


def on_device(shards, reps, hidden_acts, out_grads, momentum, kept):
    tok, rows = hidden_acts.shape
    columns = momentum.shape[2]
    chunks = columns // WIDTH
    span = min(SPAN, columns)
    spans = columns // span
    parts = span // WIDTH
    kept_count = kept.shape[0]
    tiles = WIDTH // GROUP
    lanes = tiles * kept_count
    bands = rows // GROUP
    cosines = cosine_matrix(GROUP)
    table = np.concatenate(
        [np.tile(cosines, (1, tiles)), cosines.T, np.zeros((GROUP, 128 - GROUP), np.float32)], axis=1
    )
    f32 = jnp.float32
    hbm = pl.BlockSpec(memory_space=pltpu.HBM)
    vmem = pl.BlockSpec(memory_space=pltpu.VMEM)
    in_hbm = functools.partial(pltpu.with_memory_space_constraint, memory_space=pltpu.HBM)
    kept_parts = pl.pallas_call(
        functools.partial(exchange_kernel, shards, reps, chunks, kept_count),
        out_shape=(
            jax.ShapeDtypeStruct((chunks, rows, WIDTH), f32),
            jax.ShapeDtypeStruct((chunks, rows, WIDTH), jnp.bfloat16),
            jax.ShapeDtypeStruct((parts, bands, lanes), f32),
            jax.ShapeDtypeStruct((lanes, WIDTH), f32),
            jax.ShapeDtypeStruct((GROUP, lanes), f32),
        ),
        in_specs=[hbm] * 5,
        out_specs=(vmem,) * 5,
        scratch_shapes=[
            pltpu.SMEM((kept_count,), jnp.int32),
            pltpu.VMEM(table.shape, f32),
            pltpu.VMEM((shards * tok, rows), jnp.bfloat16),
            pltpu.VMEM((rows, shards * tok), jnp.bfloat16),
            pltpu.VMEM((spans, shards * tok, span), jnp.bfloat16),
            pltpu.VMEM((chunks, bands, lanes), f32),
            pltpu.VMEM((chunks, reps, bands, lanes), f32),
            pltpu.SemaphoreType.DMA((shards + 1,)),
            pltpu.SemaphoreType.DMA((shards + 1,)),
            pltpu.SemaphoreType.DMA((spans, shards)),
            pltpu.SemaphoreType.DMA((spans, shards)),
            pltpu.SemaphoreType.DMA((chunks, reps)),
            pltpu.SemaphoreType.DMA((chunks, reps)),
            pltpu.SemaphoreType.DMA,
            pltpu.SemaphoreType.DMA,
            pltpu.SemaphoreType.DMA,
            pltpu.SemaphoreType.DMA((chunks,)),
            pltpu.SemaphoreType.DMA((chunks,)),
        ],
        compiler_params=pltpu.CompilerParams(
            collective_id=0, has_side_effects=True, vmem_limit_bytes=40 * 2**20
        ),
        name="exchange",
    )(*(in_hbm(x) for x in (kept, jnp.asarray(table), hidden_acts, out_grads, momentum)))
    return pl.pallas_call(
        store_kernel,
        out_shape=(
            jax.ShapeDtypeStruct((1, rows, columns), f32),
            jax.ShapeDtypeStruct((rows, columns), jnp.bfloat16),
        ),
        in_specs=[vmem] * 5,
        out_specs=(hbm, hbm),
        scratch_shapes=[
            pltpu.VMEM((parts, rows, WIDTH), jnp.bfloat16),
            pltpu.SemaphoreType.DMA((chunks,)),
            pltpu.SemaphoreType.DMA((chunks,)),
        ],
        compiler_params=pltpu.CompilerParams(vmem_limit_bytes=24 * 2**20),
        name="store",
    )(*kept_parts)


def solution(mesh):
    placed = (P(("rep", "shard"), None), P(("rep", "shard"), None), P("rep", None, "shard"), P())
    return jax.shard_map(
        functools.partial(on_device, mesh.shape["shard"], mesh.shape["rep"]),
        mesh=mesh,
        in_specs=placed,
        out_specs=(P("rep", None, "shard"), P(None, "shard")),
        check_vma=False,
    )
```

```python
import functools
import math

import jax
import jax.numpy as jnp
import numpy as np
from jax import lax
from jax.experimental import pallas as pl
from jax.experimental.pallas import tpu as pltpu
from jax.sharding import PartitionSpec as P

GROUP = 64
WIDTH = 256
DECAY = 0.9
MESH = pl.DeviceIdType.MESH


def cosine_matrix(length):
    frequency = np.arange(length, dtype=np.float64)[:, None]
    position = np.arange(length, dtype=np.float64)[None, :]
    cosines = np.cos(math.pi * (2.0 * position + 1.0) * frequency / (2.0 * length)) * math.sqrt(2.0 / length)
    return (cosines * np.where(frequency == 0.0, math.sqrt(0.5), 1.0)).astype(np.float32)


def flip(index, bits):
    out = index
    power = 1
    while power <= bits:
        if bits & power:
            out = out + power - 2 * power * ((index // power) % 2)
        power *= 2
    return out


def split(x):
    high = x.astype(jnp.bfloat16)
    return high, (x - high.astype(jnp.float32)).astype(jnp.bfloat16)


def dot_nt(a, b):
    return lax.dot_general(a, b, (((1,), (1,)), ((), ())), preferred_element_type=jnp.float32)


def dot_nn(a, b):
    return lax.dot_general(a, b, (((1,), (0,)), ((), ())), preferred_element_type=jnp.float32)


def decode(values, left, right_high, right_low):
    bands, lanes = values.shape
    dense = (values[:, None, :] * left[None]).reshape(bands * GROUP, lanes)
    high, low = split(dense)
    twice = jnp.concatenate([right_high, right_high], axis=0)
    return dot_nn(jnp.concatenate([high, low], axis=1), twice) + dot_nn(high, right_low)


def exchange_kernel(
    shards, reps, chunks, kept_count,
    kept_hbm, table_hbm, acts_ref, grads_ref, momentum_ref,
    residual_ref, update_ref, total_ref, right_ref, left_ref,
    kept_ref, table, acts_all, acts_t, grads_all, coeffs, gathered,
    acts_send, acts_recv, grads_send, grads_recv, rep_send, rep_recv,
    local_kept, local_table, local_acts, local_grads, local_mom,
):
    rep = lax.axis_index("rep")
    me = lax.axis_index("shard")
    core = me % 2
    tok, rows = acts_ref.shape
    columns = chunks * WIDTH
    tiles = WIDTH // GROUP
    lanes = tiles * kept_count
    chips = shards // 2
    square = chips == 4
    offsets = sorted(range(1, chips), key=lambda c: c == 2)

    load_acts = pltpu.make_async_copy(acts_ref, acts_all.at[pl.ds(0, tok), :], local_acts)
    load_kept = pltpu.make_async_copy(kept_hbm, kept_ref, local_kept)
    load_table = pltpu.make_async_copy(table_hbm, table, local_table)
    load_acts.start()

    barrier = pltpu.get_barrier_semaphore()
    for o in range(1, shards):
        pl.semaphore_signal(barrier, inc=1, device_id=(rep, flip(me, o)), device_id_type=MESH)
    for q in range(1, reps):
        pl.semaphore_signal(barrier, inc=1, device_id=(flip(rep, q), me), device_id_type=MESH)
    load_kept.start()
    load_table.start()

    def own_grads(j):
        return pltpu.make_async_copy(
            grads_ref.at[:, pl.ds(pl.multiple_of(me * columns + j * WIDTH, WIDTH), WIDTH)],
            grads_all.at[j, pl.ds(0, tok), :],
            local_grads.at[j],
        )

    def load_momentum(j):
        return pltpu.make_async_copy(
            momentum_ref.at[0, :, pl.ds(pl.multiple_of(j * WIDTH, WIDTH), WIDTH)],
            residual_ref.at[j],
            local_mom.at[j],
        )

    def send_grads(o, j):
        peer = flip(me, o)
        return pltpu.make_async_remote_copy(
            src_ref=grads_ref.at[:, pl.ds(pl.multiple_of(peer * columns + j * WIDTH, WIDTH), WIDTH)],
            dst_ref=grads_all.at[j, pl.ds(o * tok, tok), :],
            send_sem=grads_send.at[j, o],
            recv_sem=grads_recv.at[j, o],
            device_id=(rep, peer),
            device_id_type=MESH,
        )

    def start_grads(j, some):
        turns = [2 * c for c in some] + [1] + [2 * c + 1 for c in some]
        for own, order in ((0, turns), (1, turns[::-1])):
            @pl.when(core == own)
            def _():
                for o in order:
                    send_grads(o, j).start()

    def acts_copy(source, slot, bits, low, count, sem):
        own = acts_ref if source == 0 else acts_all.at[pl.ds(source * tok, tok), :]
        return pltpu.make_async_remote_copy(
            src_ref=own.at[pl.ds(low, count), :],
            dst_ref=acts_all.at[pl.ds(slot * tok + low, count), :],
            send_sem=acts_send.at[sem],
            recv_sem=acts_recv.at[sem],
            device_id=(rep, flip(me, bits)),
            device_id_type=MESH,
        )

    def send_direct(o):
        return acts_copy(0, o, o, 0, tok, o)

    def send_sibling(o):
        return acts_copy(o, o + 1, 1, 0, tok, o + 1)

    def turn(o):
        acts_t[:, pl.ds(o * tok, tok)] = acts_all[pl.ds(o * tok, tok), :].T

    def send_across(bits):
        if bits == 2:
            return acts_copy(4, 6, 2, tok // 2, tok // 2, shards)
        return acts_copy(2, 6, 4, 0, tok // 2, 6)

    def send_coeffs(q, j):
        return pltpu.make_async_remote_copy(
            src_ref=coeffs.at[j],
            dst_ref=gathered.at[j, q],
            send_sem=rep_send.at[j, q],
            recv_sem=rep_recv.at[j, q],
            device_id=(flip(rep, q), me),
            device_id_type=MESH,
        )

    direct = [c for c in offsets if not (square and c == 3)]
    pl.semaphore_wait(barrier, shards - 1 + reps - 1)
    for own, order in ((0, direct), (1, direct[::-1])):
        @pl.when(core == own)
        def _():
            for c in order:
                send_direct(2 * c).start()
    send_sibling(0).start()
    start_grads(0, offsets)
    for j in range(chunks):
        own_grads(j).start()
        load_momentum(j).start()

    load_kept.wait()
    load_table.wait()
    row = lax.broadcasted_iota(jnp.int32, (lanes, GROUP), 0) % kept_count
    freq_v = lax.broadcasted_iota(jnp.int32, (lanes, GROUP), 1)
    lane = lax.broadcasted_iota(jnp.int32, (GROUP, lanes), 1) % kept_count
    freq_u = lax.broadcasted_iota(jnp.int32, (GROUP, lanes), 0)
    hot_v = jnp.zeros((lanes, GROUP), jnp.float32)
    hot_u = jnp.zeros((GROUP, lanes), jnp.float32)
    for k in range(kept_count):
        index = kept_ref[k]
        hot_v = jnp.where((row == k) & (freq_v == index % GROUP), 1.0, hot_v)
        hot_u = jnp.where((lane == k) & (freq_u == index // GROUP), 1.0, hot_u)
    right = jnp.dot(
        hot_v, table[:, :WIDTH], precision=lax.Precision.HIGHEST, preferred_element_type=jnp.float32
    )
    same_tile = (
        lax.broadcasted_iota(jnp.int32, (lanes, WIDTH), 0) // kept_count
        == lax.broadcasted_iota(jnp.int32, (lanes, WIDTH), 1) // GROUP
    )
    right_ref[...] = jnp.where(same_tile, right, 0.0)
    left_ref[...] = jnp.dot(
        table[:, WIDTH:WIDTH + GROUP], hot_u, precision=lax.Precision.HIGHEST, preferred_element_type=jnp.float32
    )

    load_acts.wait()
    turn(0)
    for own, order in ((0, direct), (1, direct[::-1])):
        @pl.when(core == own)
        def _():
            for c in order:
                send_direct(2 * c).wait_recv()
                if square:
                    send_across(6 - 2 * c).start()
                send_sibling(2 * c).start()
    ahead = min(3, chunks)
    for j in range(1, min(2, chunks)):
        start_grads(j, offsets)
    for c in direct:
        turn(2 * c)
    for o in range(0, shards, 2):
        if not (square and o == 6):
            send_sibling(o).wait_recv()
            turn(o + 1)
    if square:
        send_across(4).wait_recv()
        send_across(2).wait_recv()
        send_sibling(6).start()
    for j in range(2, ahead):
        start_grads(j, offsets)
    if square:
        turn(6)
        send_sibling(6).wait_recv()
        turn(7)

    half = rows // 2
    bands = half // GROUP

    def finish(j, with_update):
        for q in range(1, reps):
            send_coeffs(q, j).wait_recv()
        terms = [coeffs[j]] + [gathered[j, q] for q in range(1, reps)]
        while len(terms) > 1:
            terms = [terms[i] + terms[i + 1] for i in range(0, len(terms), 2)]
        total_ref[...] = terms[0]
        if with_update:
            right_high, right_low = split(right_ref[...])
            for t in range(2):
                values = total_ref[pl.ds(t * bands, bands), :]
                update_ref[j, pl.ds(t * half, half), :] = decode(
                    values, left_ref[...], right_high, right_low
                ).astype(jnp.bfloat16)

    def chunk(j, carry):
        for o in range(1, shards):
            send_grads(o, j).wait_recv()

        @pl.when(j + ahead < chunks)
        def _():
            start_grads(j + ahead, offsets)

        own_grads(j).wait()
        load_momentum(j).wait()
        right_high, right_low = split(right_ref[...])
        right_both = jnp.concatenate([right_high, right_low], axis=0)
        left = left_ref[...]
        for t in range(2):
            part = pl.ds(t * half, half)
            gradient = dot_nn(acts_t[part, :], grads_all[j])
            value = DECAY * residual_ref[j, part, :] + gradient
            residual_ref[j, part, :] = value
            high, low = split(value)
            both = dot_nt(high, right_both)
            done = both[:, :lanes] + both[:, lanes:] + dot_nt(low, right_high)
            coeffs[j, pl.ds(t * bands, bands), :] = jnp.sum(
                done.reshape(bands, GROUP, lanes) * left[None], axis=1
            )
        for q in range(1, reps):
            send_coeffs(q, j).start()
        for t in range(2):
            part = pl.ds(t * half, half)
            values = coeffs[j, pl.ds(t * bands, bands), :]
            residual_ref[j, part, :] = residual_ref[j, part, :] - decode(values, left, right_high, right_low)

        @pl.when(j > 0)
        def _():
            finish(j - 1, True)

        return carry

    lax.fori_loop(0, chunks, chunk, 0)

    def drain(j, carry):
        for o in range(1, shards):
            send_grads(o, j).wait_send()
        return carry

    lax.fori_loop(0, chunks, drain, 0)
    for c in direct:
        send_direct(2 * c).wait_send()
    for o in range(0, shards, 2):
        send_sibling(o).wait_send()
    if square:
        send_across(2).wait_send()
        send_across(4).wait_send()
    finish(chunks - 1, False)
    for j in range(chunks):
        for q in range(1, reps):
            send_coeffs(q, j).wait_send()


def store_kernel(
    residual_ref, update_ref, total_ref, right_ref, left_ref, residual_out, update_out, last, residual_sem, update_sem
):
    chunks, rows, _ = residual_ref.shape

    def store(source, target, sem, j):
        return pltpu.make_async_copy(source, target.at[:, pl.ds(j * WIDTH, WIDTH)], sem.at[j])

    copies = [store(update_ref.at[j], update_out, update_sem, j) for j in range(chunks - 1)]
    copies += [store(residual_ref.at[j], residual_out.at[0], residual_sem, j) for j in range(chunks)]
    for copy in copies:
        copy.start()
    right_high, right_low = split(right_ref[...])
    last[...] = decode(total_ref[...], left_ref[...], right_high, right_low).astype(jnp.bfloat16)
    copies.append(store(last, update_out, update_sem, chunks - 1))
    copies[-1].start()
    for copy in copies:
        copy.wait()


def on_device(shards, reps, hidden_acts, out_grads, momentum, kept):
    tok, rows = hidden_acts.shape
    columns = momentum.shape[2]
    chunks = columns // WIDTH
    kept_count = kept.shape[0]
    tiles = WIDTH // GROUP
    lanes = tiles * kept_count
    bands = rows // GROUP
    cosines = cosine_matrix(GROUP)
    table = np.concatenate(
        [np.tile(cosines, (1, tiles)), cosines.T, np.zeros((GROUP, 128 - GROUP), np.float32)], axis=1
    )
    f32 = jnp.float32
    hbm = pl.BlockSpec(memory_space=pltpu.HBM)
    vmem = pl.BlockSpec(memory_space=pltpu.VMEM)
    in_hbm = functools.partial(pltpu.with_memory_space_constraint, memory_space=pltpu.HBM)
    kept_parts = pl.pallas_call(
        functools.partial(exchange_kernel, shards, reps, chunks, kept_count),
        out_shape=(
            jax.ShapeDtypeStruct((chunks, rows, WIDTH), f32),
            jax.ShapeDtypeStruct((chunks, rows, WIDTH), jnp.bfloat16),
            jax.ShapeDtypeStruct((bands, lanes), f32),
            jax.ShapeDtypeStruct((lanes, WIDTH), f32),
            jax.ShapeDtypeStruct((GROUP, lanes), f32),
        ),
        in_specs=[hbm] * 5,
        out_specs=(vmem,) * 5,
        scratch_shapes=[
            pltpu.SMEM((kept_count,), jnp.int32),
            pltpu.VMEM(table.shape, f32),
            pltpu.VMEM((shards * tok, rows), jnp.bfloat16),
            pltpu.VMEM((rows, shards * tok), jnp.bfloat16),
            pltpu.VMEM((chunks, shards * tok, WIDTH), jnp.bfloat16),
            pltpu.VMEM((chunks, bands, lanes), f32),
            pltpu.VMEM((chunks, reps, bands, lanes), f32),
            pltpu.SemaphoreType.DMA((shards + 1,)),
            pltpu.SemaphoreType.DMA((shards + 1,)),
            pltpu.SemaphoreType.DMA((chunks, shards)),
            pltpu.SemaphoreType.DMA((chunks, shards)),
            pltpu.SemaphoreType.DMA((chunks, reps)),
            pltpu.SemaphoreType.DMA((chunks, reps)),
            pltpu.SemaphoreType.DMA,
            pltpu.SemaphoreType.DMA,
            pltpu.SemaphoreType.DMA,
            pltpu.SemaphoreType.DMA((chunks,)),
            pltpu.SemaphoreType.DMA((chunks,)),
        ],
        compiler_params=pltpu.CompilerParams(
            collective_id=0, has_side_effects=True, vmem_limit_bytes=40 * 2**20
        ),
        name="exchange",
    )(*(in_hbm(x) for x in (kept, jnp.asarray(table), hidden_acts, out_grads, momentum)))
    return pl.pallas_call(
        store_kernel,
        out_shape=(
            jax.ShapeDtypeStruct((1, rows, columns), f32),
            jax.ShapeDtypeStruct((rows, columns), jnp.bfloat16),
        ),
        in_specs=[vmem] * 5,
        out_specs=(hbm, hbm),
        scratch_shapes=[
            pltpu.VMEM((rows, WIDTH), jnp.bfloat16),
            pltpu.SemaphoreType.DMA((chunks,)),
            pltpu.SemaphoreType.DMA((chunks,)),
        ],
        compiler_params=pltpu.CompilerParams(vmem_limit_bytes=24 * 2**20),
        name="store",
    )(*kept_parts)


def solution(mesh):
    placed = (P(("rep", "shard"), None), P(("rep", "shard"), None), P("rep", None, "shard"), P())
    return jax.shard_map(
        functools.partial(on_device, mesh.shape["shard"], mesh.shape["rep"]),
        mesh=mesh,
        in_specs=placed,
        out_specs=(P("rep", None, "shard"), P(None, "shard")),
        check_vma=False,
    )
```

```python
import functools
import math

import jax
import jax.numpy as jnp
import numpy as np
from jax import lax
from jax.experimental import pallas as pl
from jax.experimental.pallas import tpu as pltpu
from jax.sharding import PartitionSpec as P

GROUP = 64
WIDTH = 256
DECAY = 0.9
MESH = pl.DeviceIdType.MESH


def cosine_matrix(length):
    frequency = np.arange(length, dtype=np.float64)[:, None]
    position = np.arange(length, dtype=np.float64)[None, :]
    cosines = np.cos(math.pi * (2.0 * position + 1.0) * frequency / (2.0 * length)) * math.sqrt(2.0 / length)
    return (cosines * np.where(frequency == 0.0, math.sqrt(0.5), 1.0)).astype(np.float32)


def flip(index, bits):
    out = index
    power = 1
    while power <= bits:
        if bits & power:
            out = out + power - 2 * power * ((index // power) % 2)
        power *= 2
    return out


def split(x):
    high = x.astype(jnp.bfloat16)
    return high, (x - high.astype(jnp.float32)).astype(jnp.bfloat16)


def dot_nt(a, b):
    return lax.dot_general(a, b, (((1,), (1,)), ((), ())), preferred_element_type=jnp.float32)


def dot_nn(a, b):
    return lax.dot_general(a, b, (((1,), (0,)), ((), ())), preferred_element_type=jnp.float32)


def decode(values, left, right_high, right_low):
    bands, lanes = values.shape
    dense = (values[:, None, :] * left[None]).reshape(bands * GROUP, lanes)
    high, low = split(dense)
    twice = jnp.concatenate([right_high, right_high], axis=0)
    return dot_nn(jnp.concatenate([high, low], axis=1), twice) + dot_nn(high, right_low)


def exchange_kernel(
    shards, reps, chunks, kept_count,
    kept_hbm, table_hbm, acts_ref, grads_ref, momentum_ref,
    residual_ref, update_ref, total_ref, right_ref, left_ref,
    kept_ref, table, acts_all, acts_t, grads_all, coeffs, gathered,
    acts_send, acts_recv, grads_send, grads_recv, rep_send, rep_recv,
    local_kept, local_table, local_acts, local_grads, local_mom,
):
    rep = lax.axis_index("rep")
    me = lax.axis_index("shard")
    core = me % 2
    tok, rows = acts_ref.shape
    columns = chunks * WIDTH
    tiles = WIDTH // GROUP
    lanes = tiles * kept_count
    chips = shards // 2
    square = chips == 4
    offsets = sorted(range(1, chips), key=lambda c: c == 2)

    load_acts = pltpu.make_async_copy(acts_ref, acts_all.at[pl.ds(0, tok), :], local_acts)
    load_kept = pltpu.make_async_copy(kept_hbm, kept_ref, local_kept)
    load_table = pltpu.make_async_copy(table_hbm, table, local_table)
    load_acts.start()

    barrier = pltpu.get_barrier_semaphore()
    for o in range(1, shards):
        pl.semaphore_signal(barrier, inc=1, device_id=(rep, flip(me, o)), device_id_type=MESH)
    for q in range(1, reps):
        pl.semaphore_signal(barrier, inc=1, device_id=(flip(rep, q), me), device_id_type=MESH)
    load_kept.start()
    load_table.start()

    def own_grads(j):
        return pltpu.make_async_copy(
            grads_ref.at[:, pl.ds(pl.multiple_of(me * columns + j * WIDTH, WIDTH), WIDTH)],
            grads_all.at[j, pl.ds(0, tok), :],
            local_grads.at[j],
        )

    def load_momentum(j):
        return pltpu.make_async_copy(
            momentum_ref.at[0, :, pl.ds(pl.multiple_of(j * WIDTH, WIDTH), WIDTH)],
            residual_ref.at[j],
            local_mom.at[j],
        )

    def send_grads(o, j):
        peer = flip(me, o)
        return pltpu.make_async_remote_copy(
            src_ref=grads_ref.at[:, pl.ds(pl.multiple_of(peer * columns + j * WIDTH, WIDTH), WIDTH)],
            dst_ref=grads_all.at[j, pl.ds(o * tok, tok), :],
            send_sem=grads_send.at[j, o],
            recv_sem=grads_recv.at[j, o],
            device_id=(rep, peer),
            device_id_type=MESH,
        )

    def start_grads(j, some):
        turns = [2 * c for c in some] + [1] + [2 * c + 1 for c in some]
        for own, order in ((0, turns), (1, turns[::-1])):
            @pl.when(core == own)
            def _():
                for o in order:
                    send_grads(o, j).start()

    def acts_copy(source, slot, bits, low, count, sem):
        own = acts_ref if source == 0 else acts_all.at[pl.ds(source * tok, tok), :]
        return pltpu.make_async_remote_copy(
            src_ref=own.at[pl.ds(low, count), :],
            dst_ref=acts_all.at[pl.ds(slot * tok + low, count), :],
            send_sem=acts_send.at[sem],
            recv_sem=acts_recv.at[sem],
            device_id=(rep, flip(me, bits)),
            device_id_type=MESH,
        )

    def send_direct(o, part):
        return acts_copy(0, o, o, part * (tok // 2), tok // 2, o + part * (shards + 1))

    def send_sibling(o):
        return acts_copy(o, o + 1, 1, 0, tok, o + 1)

    def turn(o):
        acts_t[:, pl.ds(o * tok, tok)] = acts_all[pl.ds(o * tok, tok), :].T

    def send_across(bits):
        if bits == 2:
            return acts_copy(4, 6, 2, tok // 2, tok // 2, shards)
        return acts_copy(2, 6, 4, 0, tok // 2, 6)

    def send_coeffs(q, j):
        return pltpu.make_async_remote_copy(
            src_ref=coeffs.at[j],
            dst_ref=gathered.at[j, q],
            send_sem=rep_send.at[j, q],
            recv_sem=rep_recv.at[j, q],
            device_id=(flip(rep, q), me),
            device_id_type=MESH,
        )

    direct = [c for c in offsets if not (square and c == 3)]
    pl.semaphore_wait(barrier, shards - 1 + reps - 1)
    for own, order in ((0, direct), (1, direct[::-1])):
        @pl.when(core == own)
        def _():
            for part in range(2):
                for c in order:
                    send_direct(2 * c, part).start()
    send_sibling(0).start()
    start_grads(0, offsets)
    for j in range(chunks):
        own_grads(j).start()
        load_momentum(j).start()

    load_kept.wait()
    load_table.wait()
    row = lax.broadcasted_iota(jnp.int32, (lanes, GROUP), 0) % kept_count
    freq_v = lax.broadcasted_iota(jnp.int32, (lanes, GROUP), 1)
    lane = lax.broadcasted_iota(jnp.int32, (GROUP, lanes), 1) % kept_count
    freq_u = lax.broadcasted_iota(jnp.int32, (GROUP, lanes), 0)
    hot_v = jnp.zeros((lanes, GROUP), jnp.float32)
    hot_u = jnp.zeros((GROUP, lanes), jnp.float32)
    for k in range(kept_count):
        index = kept_ref[k]
        hot_v = jnp.where((row == k) & (freq_v == index % GROUP), 1.0, hot_v)
        hot_u = jnp.where((lane == k) & (freq_u == index // GROUP), 1.0, hot_u)
    right = jnp.dot(
        hot_v, table[:, :WIDTH], precision=lax.Precision.HIGHEST, preferred_element_type=jnp.float32
    )
    same_tile = (
        lax.broadcasted_iota(jnp.int32, (lanes, WIDTH), 0) // kept_count
        == lax.broadcasted_iota(jnp.int32, (lanes, WIDTH), 1) // GROUP
    )
    right_ref[...] = jnp.where(same_tile, right, 0.0)
    left_ref[...] = jnp.dot(
        table[:, WIDTH:WIDTH + GROUP], hot_u, precision=lax.Precision.HIGHEST, preferred_element_type=jnp.float32
    )

    load_acts.wait()
    turn(0)
    for own, order in ((0, direct), (1, direct[::-1])):
        @pl.when(core == own)
        def _():
            for c in order:
                send_direct(2 * c, 0).wait_recv()
                send_direct(2 * c, 1).wait_recv()
                if square:
                    send_across(6 - 2 * c).start()
                send_sibling(2 * c).start()
    ahead = min(3, chunks)
    for j in range(1, min(2, chunks)):
        start_grads(j, offsets)
    for c in direct:
        turn(2 * c)
    for o in range(0, shards, 2):
        if not (square and o == 6):
            send_sibling(o).wait_recv()
            turn(o + 1)
    if square:
        send_across(4).wait_recv()
        send_across(2).wait_recv()
        send_sibling(6).start()
    for j in range(2, ahead):
        start_grads(j, offsets)
    if square:
        turn(6)
        send_sibling(6).wait_recv()
        turn(7)

    half = rows // 2
    bands = half // GROUP

    def finish(j, with_update):
        for q in range(1, reps):
            send_coeffs(q, j).wait_recv()
        terms = [coeffs[j]] + [gathered[j, q] for q in range(1, reps)]
        while len(terms) > 1:
            terms = [terms[i] + terms[i + 1] for i in range(0, len(terms), 2)]
        total_ref[...] = terms[0]
        if with_update:
            right_high, right_low = split(right_ref[...])
            for t in range(2):
                values = total_ref[pl.ds(t * bands, bands), :]
                update_ref[j, pl.ds(t * half, half), :] = decode(
                    values, left_ref[...], right_high, right_low
                ).astype(jnp.bfloat16)

    def chunk(j, carry):
        for o in range(1, shards):
            send_grads(o, j).wait_recv()

        @pl.when(j + ahead < chunks)
        def _():
            start_grads(j + ahead, offsets)

        own_grads(j).wait()
        load_momentum(j).wait()
        right_high, right_low = split(right_ref[...])
        right_both = jnp.concatenate([right_high, right_low], axis=0)
        left = left_ref[...]
        for t in range(2):
            part = pl.ds(t * half, half)
            gradient = dot_nn(acts_t[part, :], grads_all[j])
            value = DECAY * residual_ref[j, part, :] + gradient
            residual_ref[j, part, :] = value
            high, low = split(value)
            both = dot_nt(high, right_both)
            done = both[:, :lanes] + both[:, lanes:] + dot_nt(low, right_high)
            coeffs[j, pl.ds(t * bands, bands), :] = jnp.sum(
                done.reshape(bands, GROUP, lanes) * left[None], axis=1
            )
        for q in range(1, reps):
            send_coeffs(q, j).start()
        for t in range(2):
            part = pl.ds(t * half, half)
            values = coeffs[j, pl.ds(t * bands, bands), :]
            residual_ref[j, part, :] = residual_ref[j, part, :] - decode(values, left, right_high, right_low)

        @pl.when(j > 0)
        def _():
            finish(j - 1, True)

        return carry

    lax.fori_loop(0, chunks, chunk, 0)

    def drain(j, carry):
        for o in range(1, shards):
            send_grads(o, j).wait_send()
        return carry

    lax.fori_loop(0, chunks, drain, 0)
    for c in direct:
        send_direct(2 * c, 0).wait_send()
        send_direct(2 * c, 1).wait_send()
    for o in range(0, shards, 2):
        send_sibling(o).wait_send()
    if square:
        send_across(2).wait_send()
        send_across(4).wait_send()
    finish(chunks - 1, False)
    for j in range(chunks):
        for q in range(1, reps):
            send_coeffs(q, j).wait_send()


def store_kernel(
    residual_ref, update_ref, total_ref, right_ref, left_ref, residual_out, update_out, last, residual_sem, update_sem
):
    chunks, rows, _ = residual_ref.shape

    def store(source, target, sem, j):
        return pltpu.make_async_copy(source, target.at[:, pl.ds(j * WIDTH, WIDTH)], sem.at[j])

    copies = [store(update_ref.at[j], update_out, update_sem, j) for j in range(chunks - 1)]
    copies += [store(residual_ref.at[j], residual_out.at[0], residual_sem, j) for j in range(chunks)]
    for copy in copies:
        copy.start()
    right_high, right_low = split(right_ref[...])
    last[...] = decode(total_ref[...], left_ref[...], right_high, right_low).astype(jnp.bfloat16)
    copies.append(store(last, update_out, update_sem, chunks - 1))
    copies[-1].start()
    for copy in copies:
        copy.wait()


def on_device(shards, reps, hidden_acts, out_grads, momentum, kept):
    tok, rows = hidden_acts.shape
    columns = momentum.shape[2]
    chunks = columns // WIDTH
    kept_count = kept.shape[0]
    tiles = WIDTH // GROUP
    lanes = tiles * kept_count
    bands = rows // GROUP
    cosines = cosine_matrix(GROUP)
    table = np.concatenate(
        [np.tile(cosines, (1, tiles)), cosines.T, np.zeros((GROUP, 128 - GROUP), np.float32)], axis=1
    )
    f32 = jnp.float32
    hbm = pl.BlockSpec(memory_space=pltpu.HBM)
    vmem = pl.BlockSpec(memory_space=pltpu.VMEM)
    in_hbm = functools.partial(pltpu.with_memory_space_constraint, memory_space=pltpu.HBM)
    kept_parts = pl.pallas_call(
        functools.partial(exchange_kernel, shards, reps, chunks, kept_count),
        out_shape=(
            jax.ShapeDtypeStruct((chunks, rows, WIDTH), f32),
            jax.ShapeDtypeStruct((chunks, rows, WIDTH), jnp.bfloat16),
            jax.ShapeDtypeStruct((bands, lanes), f32),
            jax.ShapeDtypeStruct((lanes, WIDTH), f32),
            jax.ShapeDtypeStruct((GROUP, lanes), f32),
        ),
        in_specs=[hbm] * 5,
        out_specs=(vmem,) * 5,
        scratch_shapes=[
            pltpu.SMEM((kept_count,), jnp.int32),
            pltpu.VMEM(table.shape, f32),
            pltpu.VMEM((shards * tok, rows), jnp.bfloat16),
            pltpu.VMEM((rows, shards * tok), jnp.bfloat16),
            pltpu.VMEM((chunks, shards * tok, WIDTH), jnp.bfloat16),
            pltpu.VMEM((chunks, bands, lanes), f32),
            pltpu.VMEM((chunks, reps, bands, lanes), f32),
            pltpu.SemaphoreType.DMA((2 * shards + 1,)),
            pltpu.SemaphoreType.DMA((2 * shards + 1,)),
            pltpu.SemaphoreType.DMA((chunks, shards)),
            pltpu.SemaphoreType.DMA((chunks, shards)),
            pltpu.SemaphoreType.DMA((chunks, reps)),
            pltpu.SemaphoreType.DMA((chunks, reps)),
            pltpu.SemaphoreType.DMA,
            pltpu.SemaphoreType.DMA,
            pltpu.SemaphoreType.DMA,
            pltpu.SemaphoreType.DMA((chunks,)),
            pltpu.SemaphoreType.DMA((chunks,)),
        ],
        compiler_params=pltpu.CompilerParams(
            collective_id=0, has_side_effects=True, vmem_limit_bytes=40 * 2**20
        ),
        name="exchange",
    )(*(in_hbm(x) for x in (kept, jnp.asarray(table), hidden_acts, out_grads, momentum)))
    return pl.pallas_call(
        store_kernel,
        out_shape=(
            jax.ShapeDtypeStruct((1, rows, columns), f32),
            jax.ShapeDtypeStruct((rows, columns), jnp.bfloat16),
        ),
        in_specs=[vmem] * 5,
        out_specs=(hbm, hbm),
        scratch_shapes=[
            pltpu.VMEM((rows, WIDTH), jnp.bfloat16),
            pltpu.SemaphoreType.DMA((chunks,)),
            pltpu.SemaphoreType.DMA((chunks,)),
        ],
        compiler_params=pltpu.CompilerParams(vmem_limit_bytes=24 * 2**20),
        name="store",
    )(*kept_parts)


def solution(mesh):
    placed = (P(("rep", "shard"), None), P(("rep", "shard"), None), P("rep", None, "shard"), P())
    return jax.shard_map(
        functools.partial(on_device, mesh.shape["shard"], mesh.shape["rep"]),
        mesh=mesh,
        in_specs=placed,
        out_specs=(P("rep", None, "shard"), P(None, "shard")),
        check_vma=False,
    )
```
